32 devices in a mesh: ctx: 8 (over y, x, core), tp: 4 (over z).
Axes of the slice: x: 2, y: 2, z: 4, core: 2. Of those that a mesh axis runs over, the one named last changes fastest.
Arguments:
- hidden: bfloat16 [2048, 5120], P('ctx', 'tp'), may hold values from -6 to 6
- queries: bfloat16 [2048, 5120], P('ctx', 'tp'), may hold values from -28 to 28
- key_weight: bfloat16 [5120, 1024], P(None, 'tp'), may hold values from -0.078125 to 0.078125
- value_weight: bfloat16 [5120, 1024], P(None, 'tp'), may hold values from -0.078125 to 0.078125
- parents: int32 [16], replicated, may hold values from -1 to 14, as said below
- upstream: bfloat16 [2048, 5120], P('ctx', 'tp'), may hold values from -6 to 6
Outputs:
- attention: bfloat16 [2048, 5120], P('ctx', 'tp')
- query_grad: bfloat16 [2048, 5120], P('ctx', 'tp')
- hidden_grad: bfloat16 [2048, 5120], P('ctx', 'tp')
- key_weight_grad: float32 [5120, 1024], P('ctx', 'tp')
- value_weight_grad: float32 [5120, 1024], P('ctx', 'tp')
The draws below stay inside these ranges and needn't reach their ends.
Inputs may be any that keep to these rules, and one draw needn't show every extreme that they name: Node blocks lie in depth-first order: parents[b] < b is the parent of block b for b > 0, parents[0] = -1 and block 0 is the only root; no root-to-leaf path holds more than 8 blocks; the last 7 blocks form one chain below block 0, so that the last block's path holds exactly 8 blocks.
All inputs are finite; a program needn't handle non-finite values.
Results may differ from the reference program's by a relative error of at most 0.023.
The reference program's roundings to bfloat16 on the way count: a program that leaves them out, or rounds other values in their place, can miss the bound.
Values may be sent and summed in bfloat16 or wider, within the bound.
A program may use at most 128 MiB of HBM per device.

```python
import math
import jax
import jax.numpy as jnp
from jax import lax

D = 5120
QH = 40
KVH = 8
HD = 128
BLOCK = 128
DEPTH = 8
NBLK = 16
TOKENS = 2048
N_TP = 4


def draw_parents(key, part):
    coin_key = jax.random.fold_in(key, 1)
    jump_key = jax.random.fold_in(key, 2)
    coin_flips = jax.random.randint(coin_key, (NBLK,), 0, 4, dtype=jnp.int32)
    jump_draws = jax.random.randint(jump_key, (NBLK,), 0, 1 << 20, dtype=jnp.int32)
    forced_start = NBLK - DEPTH + 1

    def advance(previous, inputs):
        position, coin_flip, jump_draw = inputs
        deeper = jnp.minimum(previous + 1, DEPTH - 1)
        jumped = 1 + jump_draw % jnp.maximum(deeper, 1)
        forced = position >= forced_start
        chosen = jnp.where(coin_flip < 2, deeper, jumped)
        chosen = jnp.where(forced, position - forced_start + 1, chosen)
        chosen = jnp.where(position == 0, 0, chosen).astype(jnp.int32)
        return (chosen, chosen)
    positions = jnp.arange(NBLK, dtype=jnp.int32)
    final_depth, depths = lax.scan(advance, jnp.int32(0), (positions, coin_flips, jump_draws))
    earlier = positions[None, :] < positions[:, None]
    matches = earlier & (depths[None, :] == depths[:, None] - 1)
    return jnp.max(jnp.where(matches, positions[None, :], -1), axis=1).astype(jnp.int32)


def draw_queries(key, part):
    base_key = jax.random.fold_in(key, 5)
    return jnp.clip(jax.random.normal(base_key, (TOKENS, QH * HD), jnp.float32), -6.0, 6.0).astype(jnp.bfloat16)


def raised(entries, own_key, source, target, blocks, factor):
    def block_of(dim):
        return (jnp.arange(entries.shape[dim]) // (entries.shape[dim] // blocks)).reshape((-1,) + (1,) * (entries.ndim - 1 - dim))

    first = jax.random.permutation(own_key, blocks)[block_of(target)]
    far = (block_of(target) + blocks // 2) % blocks
    return jnp.where((block_of(source) == first) | (block_of(source) == far), factor * entries, entries)


def block_levels(own_key, extent, split, smallest, largest):
    gain, own = 1.0, jax.random.fold_in(own_key, 6)
    for dim, shards_of in split:
        draws = jnp.exp(jax.random.uniform(jax.random.fold_in(own, dim), (shards_of,), jnp.float32, smallest / len(split), largest / len(split)))
        gain = gain * jnp.repeat(draws, extent[dim] // shards_of).reshape([-1 if axis == dim else 1 for axis in range(len(extent))])
    return gain


def gaussian(own_key, extent, width, bound, pieces=(), held_as=jnp.bfloat16):
    factor_of = block_levels(own_key, extent, pieces, -0.22, 0.18) if pieces else 1.0
    values = jax.random.normal(own_key, extent, jnp.float32) * width * factor_of
    return jnp.minimum(jnp.maximum(values, -bound), bound).astype(held_as)


def heavy_noise(key, shape, scale, most, shards, heavy, kind=jnp.bfloat16):
    array = scale * jax.random.normal(key, shape, jnp.float32)
    if shards:
        array = array * block_levels(key, shape, shards, -0.22, 0.18)
    return jnp.clip(raised(array, jax.random.fold_in(key, 3), *heavy), -most, most).astype(kind)


def setup_inputs(seed: int = 0) -> dict:
    key_of = jax.random.split(jax.random.key(seed), 7)
    hidden = heavy_noise(key_of[0], (TOKENS, D), 1.0, 6.0, ((0, 8), (1, 4)), (0, 1, 8, 2.0))
    queries = draw_queries(jax.random.fold_in(key_of[6], 71), 0)
    key_weight = gaussian(key_of[2], (D, KVH * HD), D ** -0.5, 0.078125, ((1, 4),))
    value_weight = gaussian(key_of[3], (D, KVH * HD), D ** -0.5, 0.078125, ((1, 4),))
    parents = draw_parents(jax.random.fold_in(key_of[6], 71), 0)
    upstream = gaussian(key_of[5], (TOKENS, QH * HD), 1.0, 6.0, ((0, 8), (1, 4)))
    return {"hidden": hidden, "queries": queries, "key_weight": key_weight, "value_weight": value_weight, "parents": parents, "upstream": upstream}


THETA = 1000000.0
NEGATIVE = -1e+30
HIGHEST = lax.Precision.HIGHEST

def tree_tables(parents, block_total, depth_slots):
    indices = jnp.arange(block_total, dtype=jnp.int32)
    parent_link = (parents[:, None] == indices[None, :]).astype(jnp.float32)
    closure = jnp.eye(block_total, dtype=jnp.float32) + parent_link
    for repeat in range(depth_slots.bit_length()):
        closure = jnp.minimum(jnp.dot(closure, closure, precision=HIGHEST, preferred_element_type=jnp.float32), 1.0)
    closure_int = closure.astype(jnp.int32)
    depths = (lax.optimization_barrier(jnp.sum(closure_int, axis=1)) - 1).astype(jnp.int32)
    levels = jnp.arange(depth_slots, dtype=jnp.int32)
    select = closure_int[:, :, None] * (depths[None, :, None] == levels[None, None, :]).astype(jnp.int32)
    path_ids = (lax.optimization_barrier(jnp.sum(select * indices[None, :, None], axis=1)) + lax.optimization_barrier(jnp.sum(select, axis=1)) - 1).astype(jnp.int32)
    return (depths, path_ids)

def rope_angles(depths, block_len, head_width):
    offset = jnp.arange(block_len, dtype=jnp.int32)
    position = (depths[:, None] * block_len + offset[None, :]).astype(jnp.float32)
    midpoint = head_width // 2
    frequency = jnp.exp(jnp.arange(midpoint, dtype=jnp.float32) * (-2.0 * math.log(THETA) / head_width))
    angles = position[:, :, None] * frequency[None, None, :]
    return (jnp.cos(angles), jnp.sin(angles))

def rotate_pairs(fields, cosine, sine_table, direction):
    midpoint = fields.shape[-1] // 2
    leading = fields[..., :midpoint]
    trailing = fields[..., midpoint:]
    cos_part = cosine[:, :, None, :]
    sin_part = direction * sine_table[:, :, None, :]
    return jnp.concatenate([leading * cos_part - trailing * sin_part, trailing * cos_part + leading * sin_part], axis=-1)

def allowed_mask(depths, block_len, slot_count):
    query_pos = jnp.arange(block_len, dtype=jnp.int32)
    key_index = jnp.arange(slot_count * block_len, dtype=jnp.int32)
    key_slot = key_index // block_len
    key_offset = key_index % block_len
    earlier = key_slot[None, None, :] < depths[:, None, None]
    itself = (key_slot[None, None, :] == depths[:, None, None]) & (key_offset[None, None, :] <= query_pos[None, :, None])
    return earlier | itself

def attend_reference(query_blocks, key_rows, value_rows, allowed, upstream_blocks, score_scale):
    query_float = query_blocks.astype(jnp.float32)
    key_float = key_rows.astype(jnp.float32)
    value_float = value_rows.astype(jnp.float32)
    upstream_float = upstream_blocks.astype(jnp.float32)
    scores = jnp.einsum('bqhgd,bkhd->bhgqk', query_float, key_float, precision=HIGHEST) * score_scale
    scores = jnp.where(allowed[:, None, None], scores, NEGATIVE)
    maximum = lax.optimization_barrier(jnp.max(scores, axis=-1, keepdims=True))
    weights = jnp.exp(scores - maximum)
    totals = lax.optimization_barrier(jnp.sum(weights, axis=-1, keepdims=True))
    weights_round = lax.optimization_barrier(weights.astype(jnp.bfloat16)).astype(jnp.float32)
    mixed_rows = jnp.einsum('bhgqk,bkhd->bqhgd', weights_round, value_float, precision=HIGHEST)
    totals_rows = jnp.transpose(totals, (0, 3, 1, 2, 4))
    output = (mixed_rows / totals_rows).astype(jnp.bfloat16)
    output_float = lax.optimization_barrier(output).astype(jnp.float32)
    logsum = maximum + jnp.log(totals)
    deltas = jnp.transpose(lax.optimization_barrier(jnp.sum(upstream_float * output_float, axis=-1)), (0, 2, 3, 1))[..., None]
    probabilities = jnp.exp(scores - logsum)
    prob_round = lax.optimization_barrier(probabilities.astype(jnp.bfloat16)).astype(jnp.float32)
    value_grad = jnp.einsum('bhgqk,bqhgd->bkhd', prob_round, upstream_float, precision=HIGHEST)
    prob_grad = jnp.einsum('bqhgd,bkhd->bhgqk', upstream_float, value_float, precision=HIGHEST)
    score_grad = lax.optimization_barrier((probabilities * (prob_grad - deltas)).astype(jnp.bfloat16)).astype(jnp.float32)
    query_grad = (jnp.einsum('bhgqk,bkhd->bqhgd', score_grad, key_float, precision=HIGHEST) * score_scale).astype(jnp.bfloat16)
    key_grad = jnp.einsum('bhgqk,bqhgd->bkhd', score_grad, query_float, precision=HIGHEST) * score_scale
    return (output, query_grad, key_grad, value_grad)

def reference(hidden, queries, key_weight, value_weight, parents, upstream):
    groups = QH // KVH
    key_width = KVH * HD
    pair_width = 2 * key_width
    score_scale = 1.0 / math.sqrt(HD)
    depth_all, path_all = tree_tables(parents, NBLK, DEPTH)
    cosine, sine_table = rope_angles(depth_all, BLOCK, HD)
    key_linear = jnp.dot(hidden, key_weight, preferred_element_type=jnp.float32).reshape(NBLK, BLOCK, KVH, HD)
    key_rotated = rotate_pairs(key_linear, cosine, sine_table, 1.0).astype(jnp.bfloat16).reshape(NBLK, BLOCK, key_width)
    value_rows = jnp.dot(hidden, value_weight, preferred_element_type=jnp.float32).astype(jnp.bfloat16).reshape(NBLK, BLOCK, key_width)
    key_value = jnp.concatenate([key_rotated, value_rows], axis=-1)
    query_all = queries.reshape(NBLK, BLOCK, KVH, groups, HD)
    upstream_all = upstream.reshape(NBLK, BLOCK, KVH, groups, HD)

    def visit(accumulated, block_id):
        path_ids = jnp.clip(path_all[block_id], 0, NBLK - 1).astype(jnp.int32)
        slot_rows = key_value[path_ids].reshape(1, DEPTH * BLOCK, pair_width)
        key_part = slot_rows[..., :key_width].reshape(1, DEPTH * BLOCK, KVH, HD)
        value_part = slot_rows[..., key_width:].reshape(1, DEPTH * BLOCK, KVH, HD)
        allowed = allowed_mask(depth_all[block_id][None], BLOCK, DEPTH)
        output, query_grad, key_grad, value_grad = attend_reference(query_all[block_id][None], key_part, value_part, allowed, upstream_all[block_id][None], score_scale)
        slot_grads = jnp.concatenate([key_grad.reshape(DEPTH, BLOCK, key_width), value_grad.reshape(DEPTH, BLOCK, key_width)], axis=-1)
        accumulated = accumulated.at[path_ids].add(slot_grads)
        return (accumulated, (output[0], query_grad[0]))
    start_grads = jnp.zeros((NBLK, BLOCK, pair_width), jnp.float32)
    pair_grads, outputs = lax.scan(visit, start_grads, jnp.arange(NBLK, dtype=jnp.int32))
    attention = outputs[0].reshape(TOKENS, QH * HD)
    query_grad = outputs[1].reshape(TOKENS, QH * HD)
    key_total = pair_grads[..., :key_width].reshape(NBLK, BLOCK, KVH, HD)
    key_linear_grad = rotate_pairs(key_total, cosine, sine_table, -1.0).astype(jnp.bfloat16).reshape(TOKENS, key_width)
    value_grad_rows = pair_grads[..., key_width:].reshape(TOKENS, key_width).astype(jnp.bfloat16)
    key_weight_grad = jnp.dot(hidden.T, key_linear_grad, preferred_element_type=jnp.float32)
    value_weight_grad = jnp.dot(hidden.T, value_grad_rows, preferred_element_type=jnp.float32)
    share_width = key_width // N_TP
    total_grad = jnp.zeros((TOKENS, D), jnp.float32)
    for member in range(N_TP):
        low_col = member * share_width
        high_col = low_col + share_width
        partial_rows = jnp.dot(key_linear_grad[:, low_col:high_col], key_weight[:, low_col:high_col].T, preferred_element_type=jnp.float32)
        partial_rows = partial_rows + jnp.dot(value_grad_rows[:, low_col:high_col], value_weight[:, low_col:high_col].T, preferred_element_type=jnp.float32)
        total_grad = total_grad + lax.optimization_barrier(partial_rows.astype(jnp.bfloat16)).astype(jnp.float32)
    hidden_grad = total_grad.astype(jnp.bfloat16)
    return (attention, query_grad, hidden_grad, key_weight_grad, value_weight_grad)
```

```python
import math

import jax
import jax.numpy as jnp
from jax import lax
from jax.experimental import pallas as pl
from jax.experimental.pallas import tpu as pltpu
from jax.sharding import PartitionSpec as P

HD = 128
BLOCK = 128
DEPTH = 8
THETA = 1000000.0
NEGATIVE = -1e30
VMEM_LIMIT = 56 * 1024 * 1024
MESH = pl.DeviceIdType.MESH


def walk(parents_ref, block):
    chain = [block]
    for _ in range(DEPTH - 1):
        last = chain[-1]
        above = parents_ref[jnp.maximum(last, 0)]
        chain.append(jnp.where(last > 0, above, -1))
    depth = jnp.int32(0)
    for node in chain[1:]:
        depth = depth + jnp.where(node >= 0, 1, 0)
    path = []
    for level in range(DEPTH):
        found = jnp.int32(0)
        for hop in range(DEPTH):
            found = found + jnp.where(depth - hop == level, chain[hop], 0)
        path.append(found)
    return depth, path


def dot_f32(left, right, left_dim, right_dim):
    return lax.dot_general(
        left, right, (((left_dim,), (right_dim,)), ((), ())), preferred_element_type=jnp.float32
    )


def attend(parents_ref, kv_ref, q_ref, u_ref, att_ref, qg_ref, part_ref, s_ref, grads_ref):
    rows, width = q_ref.shape
    blocks = rows // BLOCK
    pair_width = kv_ref.shape[1]
    key_width = pair_width // 2
    key_heads = key_width // HD
    groups = width // key_width
    lanes = groups * BLOCK
    step = 2 * BLOCK
    steps = DEPTH // 2
    scale = 1.0 / math.sqrt(HD)
    first = lax.axis_index("ctx") * blocks

    def one_block(b, carry):
        depth, path = walk(parents_ref, first + b)
        row0 = pl.multiple_of(b * BLOCK, BLOCK)
        here = pl.ds(row0, BLOCK)
        key_row = lax.broadcasted_iota(jnp.int32, (step, lanes), 0)
        query_row = lax.broadcasted_iota(jnp.int32, (step, lanes), 1) % BLOCK
        limit = depth * BLOCK + query_row - key_row
        for g in range(key_heads):
            def head_cols(h):
                return slice((g * groups + h) * HD, (g * groups + h + 1) * HD)

            key_cols = slice(g * HD, (g + 1) * HD)
            value_cols = slice(key_width + g * HD, key_width + (g + 1) * HD)
            q = jnp.concatenate([q_ref[here, head_cols(h)] for h in range(groups)], axis=0)
            u = jnp.concatenate([u_ref[here, head_cols(h)] for h in range(groups)], axis=0)
            u_t = u.astype(jnp.float32).T

            def pair(p, cols):
                return jnp.concatenate(
                    [
                        kv_ref[pl.ds(pl.multiple_of(path[2 * p + i] * BLOCK, BLOCK), BLOCK), cols]
                        for i in range(2)
                    ],
                    axis=0,
                )

            top = jnp.full((1, lanes), NEGATIVE, jnp.float32)
            for p in range(steps):
                s = dot_f32(pair(p, key_cols), q, 1, 1) * scale
                s = jnp.where(limit >= p * step, s, NEGATIVE)
                s_ref[p] = s
                top = jnp.maximum(top, jnp.max(s, axis=0, keepdims=True))
            totals = jnp.zeros((1, lanes), jnp.float32)
            mixed = jnp.zeros((HD, lanes), jnp.float32)
            for p in range(steps):
                w = jnp.exp(s_ref[p] - top)
                s_ref[p] = w
                totals = totals + jnp.sum(w, axis=0, keepdims=True)
                mixed = mixed + dot_f32(pair(p, value_cols), w.astype(jnp.bfloat16), 0, 0)
            out_t = (mixed / totals).astype(jnp.bfloat16).astype(jnp.float32)
            out = out_t.T.astype(jnp.bfloat16)
            for h in range(groups):
                att_ref[here, head_cols(h)] = out[h * BLOCK : (h + 1) * BLOCK]
            deltas = jnp.sum(out_t * u_t, axis=0, keepdims=True)
            inverse = 1.0 / totals
            query_grad = jnp.zeros((HD, lanes), jnp.float32)
            for p in range(steps):
                prob = s_ref[p] * inverse
                value_part = dot_f32(prob.astype(jnp.bfloat16), u, 1, 0)
                prob_grad = dot_f32(pair(p, value_cols), u, 1, 1)
                ds = (prob * (prob_grad - deltas)).astype(jnp.bfloat16)
                key_part = dot_f32(ds, q, 1, 0) * scale
                query_grad = query_grad + dot_f32(pair(p, key_cols), ds, 0, 0)
                for i in range(2):
                    grads_ref[b, 2 * p + i, :, key_cols] = key_part[i * BLOCK : (i + 1) * BLOCK]
                    grads_ref[b, 2 * p + i, :, value_cols] = value_part[i * BLOCK : (i + 1) * BLOCK]
            qg = (query_grad * scale).T.astype(jnp.bfloat16)
            for h in range(groups):
                qg_ref[here, head_cols(h)] = qg[h * BLOCK : (h + 1) * BLOCK]
        return carry

    lax.fori_loop(0, blocks, one_block, 0)

    paths = [walk(parents_ref, first + b) for b in range(blocks)]
    block_total = part_ref.shape[0] // BLOCK

    def one_target(target, carry):
        total = jnp.zeros((BLOCK, pair_width), jnp.float32)
        for b in range(blocks):
            depth, path = paths[b]
            slot = jnp.int32(0)
            hits = jnp.int32(0)
            for level in range(DEPTH):
                hit = jnp.where((path[level] == target) & (depth >= level), 1, 0)
                slot = slot + hit * level
                hits = hits + hit
            total = total + jnp.where(hits > 0, grads_ref[b, slot], 0.0)
        part_ref[pl.ds(pl.multiple_of(target * BLOCK, BLOCK), BLOCK), :] = total.astype(
            part_ref.dtype
        )
        return carry

    lax.fori_loop(0, block_total, one_target, 0)


def attention_call(parents, kv, queries, upstream, part_dtype):
    rows, width = queries.shape
    blocks = rows // BLOCK
    pair_width = kv.shape[1]
    groups = width // (pair_width // 2)
    vmem = pl.BlockSpec(memory_space=pltpu.VMEM)
    return pl.pallas_call(
        attend,
        name="attend",
        out_shape=(
            jax.ShapeDtypeStruct(queries.shape, jnp.bfloat16),
            jax.ShapeDtypeStruct(queries.shape, jnp.bfloat16),
            jax.ShapeDtypeStruct(kv.shape, part_dtype),
        ),
        in_specs=[pl.BlockSpec(memory_space=pltpu.SMEM), vmem, vmem, vmem],
        out_specs=(vmem, vmem, vmem),
        scratch_shapes=[
            pltpu.VMEM((DEPTH // 2, 2 * BLOCK, groups * BLOCK), jnp.float32),
            pltpu.VMEM((blocks, DEPTH, BLOCK, pair_width), jnp.float32),
        ],
        compiler_params=pltpu.CompilerParams(vmem_limit_bytes=VMEM_LIMIT),
    )(parents, kv, queries, upstream)


def depths_of(parents, block_total):
    node = jnp.arange(block_total, dtype=jnp.int32)
    depths = jnp.zeros((block_total,), jnp.int32)
    link = (jnp.arange(block_total, dtype=jnp.int32)[None, :], parents[None, :])
    for _ in range(DEPTH - 1):
        above = jnp.sum(jnp.where(node[:, None] == link[0], link[1], 0), axis=1)
        node = jnp.where(node > 0, above, -1)
        depths = depths + (node >= 0).astype(jnp.int32)
    return depths


def rope_rows(depths):
    position = (depths[:, None] * BLOCK + jnp.arange(BLOCK, dtype=jnp.int32)).reshape(-1)
    frequency = jnp.exp(
        jnp.arange(HD // 2, dtype=jnp.float32) * (-2.0 * math.log(THETA) / HD)
    )
    angles = position.astype(jnp.float32)[:, None] * frequency[None, :]
    return jnp.cos(angles), jnp.sin(angles)


def rotate(rows, cosine, sine):
    heads = rows.reshape(rows.shape[0], -1, 2, HD // 2)
    lead, trail = heads[:, :, 0], heads[:, :, 1]
    c, s = cosine[:, None, :], sine[:, None, :]
    return jnp.stack([lead * c - trail * s, trail * c + lead * s], axis=2).reshape(rows.shape)


def shards(hidden, queries, key_weight, value_weight, parents, upstream):
    rows = hidden.shape[0]
    blocks = rows // BLOCK
    key_width = key_weight.shape[1]
    block_total = parents.shape[0]
    depths = lax.dynamic_slice_in_dim(
        depths_of(parents, block_total), lax.axis_index("ctx") * blocks, blocks, 0
    )
    cosine, sine = rope_rows(depths)
    features = lax.all_gather(hidden, "tp", axis=1, tiled=True)
    hidden_columns = lax.all_to_all(features, "ctx", split_axis=1, concat_axis=0, tiled=True)
    key_linear = jnp.dot(features, key_weight, preferred_element_type=jnp.float32)
    keys = rotate(key_linear, cosine, sine).astype(jnp.bfloat16)
    values = jnp.dot(features, value_weight, preferred_element_type=jnp.float32).astype(
        jnp.bfloat16
    )
    kv = lax.all_gather(jnp.concatenate([keys, values], axis=1), "ctx", axis=0, tiled=True)
    attention, query_grad, part = attention_call(parents, kv, queries, upstream, jnp.float32)
    own = lax.psum_scatter(part, "ctx", scatter_dimension=0, tiled=True)
    key_grad = rotate(own[:, :key_width], cosine, -sine).astype(jnp.bfloat16)
    value_grad = own[:, key_width:].astype(jnp.bfloat16)
    grads = lax.all_gather(
        jnp.concatenate([key_grad, value_grad], axis=1), "ctx", axis=0, tiled=True
    )
    weight_grads = lax.dot_general(
        hidden_columns, grads, (((0,), (0,)), ((), ())), preferred_element_type=jnp.float32
    )
    partial = dot_f32(key_grad, key_weight, 1, 1) + dot_f32(value_grad, value_weight, 1, 1)
    hidden_grad = lax.psum_scatter(
        partial.astype(jnp.bfloat16), "tp", scatter_dimension=1, tiled=True
    )
    return (
        attention,
        query_grad,
        hidden_grad,
        weight_grads[:, :key_width],
        weight_grads[:, key_width:],
    )


def solution(mesh):
    return jax.shard_map(
        shards,
        mesh=mesh,
        in_specs=(
            P("ctx", "tp"),
            P("ctx", "tp"),
            P(None, "tp"),
            P(None, "tp"),
            P(),
            P("ctx", "tp"),
        ),
        out_specs=(P("ctx", "tp"),) * 5,
        check_vma=False,
    )
```

```python
from functools import partial
import math

import jax
import jax.numpy as jnp
from jax import lax
from jax.experimental import pallas as pl
from jax.experimental.pallas import tpu as pltpu
from jax.sharding import PartitionSpec as P

HD = 128
BLOCK = 128
DEPTH = 8
THETA = 1000000.0
NEGATIVE = -1e30
VMEM_LIMIT = 56 * 1024 * 1024
MESH = pl.DeviceIdType.MESH


def walk(parents_ref, block):
    chain = [block]
    for _ in range(DEPTH - 1):
        last = chain[-1]
        above = parents_ref[jnp.maximum(last, 0)]
        chain.append(jnp.where(last > 0, above, -1))
    depth = jnp.int32(0)
    for node in chain[1:]:
        depth = depth + jnp.where(node >= 0, 1, 0)
    path = []
    for level in range(DEPTH):
        found = jnp.int32(0)
        for hop in range(DEPTH):
            found = found + jnp.where(depth - hop == level, chain[hop], 0)
        path.append(found)
    return depth, path


def dot_f32(left, right, left_dim, right_dim):
    return lax.dot_general(
        left, right, (((left_dim,), (right_dim,)), ((), ())), preferred_element_type=jnp.float32
    )


def attend(parents_ref, kv_ref, q_ref, u_ref, att_ref, qg_ref, part_ref, s_ref, grads_ref):
    rows, width = q_ref.shape
    blocks = rows // BLOCK
    pair_width = kv_ref.shape[1]
    key_width = pair_width // 2
    key_heads = key_width // HD
    groups = width // key_width
    lanes = groups * BLOCK
    step = 2 * BLOCK
    steps = DEPTH // 2
    scale = 1.0 / math.sqrt(HD)
    first = lax.axis_index("ctx") * blocks

    def one_block(b, carry):
        depth, path = walk(parents_ref, first + b)
        row0 = pl.multiple_of(b * BLOCK, BLOCK)
        here = pl.ds(row0, BLOCK)
        key_row = lax.broadcasted_iota(jnp.int32, (step, lanes), 0)
        query_row = lax.broadcasted_iota(jnp.int32, (step, lanes), 1) % BLOCK
        limit = depth * BLOCK + query_row - key_row
        for g in range(key_heads):
            def head_cols(h):
                return slice((g * groups + h) * HD, (g * groups + h + 1) * HD)

            key_cols = slice(g * HD, (g + 1) * HD)
            value_cols = slice(key_width + g * HD, key_width + (g + 1) * HD)
            q = jnp.concatenate([q_ref[here, head_cols(h)] for h in range(groups)], axis=0)
            u = jnp.concatenate([u_ref[here, head_cols(h)] for h in range(groups)], axis=0)
            u_t = u.astype(jnp.float32).T

            def pair(p, cols):
                return jnp.concatenate(
                    [
                        kv_ref[pl.ds(pl.multiple_of(path[2 * p + i] * BLOCK, BLOCK), BLOCK), cols]
                        for i in range(2)
                    ],
                    axis=0,
                )

            top = jnp.full((1, lanes), NEGATIVE, jnp.float32)
            for p in range(steps):
                s = dot_f32(pair(p, key_cols), q, 1, 1) * scale
                s = jnp.where(limit >= p * step, s, NEGATIVE)
                s_ref[p] = s
                top = jnp.maximum(top, jnp.max(s, axis=0, keepdims=True))
            totals = jnp.zeros((1, lanes), jnp.float32)
            mixed = jnp.zeros((HD, lanes), jnp.float32)
            for p in range(steps):
                w = jnp.exp(s_ref[p] - top)
                s_ref[p] = w
                totals = totals + jnp.sum(w, axis=0, keepdims=True)
                mixed = mixed + dot_f32(pair(p, value_cols), w.astype(jnp.bfloat16), 0, 0)
            out_t = (mixed / totals).astype(jnp.bfloat16).astype(jnp.float32)
            out = out_t.T.astype(jnp.bfloat16)
            for h in range(groups):
                att_ref[here, head_cols(h)] = out[h * BLOCK : (h + 1) * BLOCK]
            deltas = jnp.sum(out_t * u_t, axis=0, keepdims=True)
            inverse = 1.0 / totals
            query_grad = jnp.zeros((HD, lanes), jnp.float32)
            for p in range(steps):
                prob = s_ref[p] * inverse
                value_part = dot_f32(prob.astype(jnp.bfloat16), u, 1, 0)
                prob_grad = dot_f32(pair(p, value_cols), u, 1, 1)
                ds = (prob * (prob_grad - deltas)).astype(jnp.bfloat16)
                key_part = dot_f32(ds, q, 1, 0) * scale
                query_grad = query_grad + dot_f32(pair(p, key_cols), ds, 0, 0)
                for i in range(2):
                    grads_ref[b, 2 * p + i, :, key_cols] = key_part[i * BLOCK : (i + 1) * BLOCK]
                    grads_ref[b, 2 * p + i, :, value_cols] = value_part[i * BLOCK : (i + 1) * BLOCK]
            qg = (query_grad * scale).T.astype(jnp.bfloat16)
            for h in range(groups):
                qg_ref[here, head_cols(h)] = qg[h * BLOCK : (h + 1) * BLOCK]
        return carry

    lax.fori_loop(0, blocks, one_block, 0)

    paths = [walk(parents_ref, first + b) for b in range(blocks)]
    block_total = part_ref.shape[0] // BLOCK

    def one_target(target, carry):
        total = jnp.zeros((BLOCK, pair_width), jnp.float32)
        for b in range(blocks):
            depth, path = paths[b]
            slot = jnp.int32(0)
            hits = jnp.int32(0)
            for level in range(DEPTH):
                hit = jnp.where((path[level] == target) & (depth >= level), 1, 0)
                slot = slot + hit * level
                hits = hits + hit
            total = total + jnp.where(hits > 0, grads_ref[b, slot], 0.0)
        part_ref[pl.ds(pl.multiple_of(target * BLOCK, BLOCK), BLOCK), :] = total.astype(
            part_ref.dtype
        )
        return carry

    lax.fori_loop(0, block_total, one_target, 0)


def attention_call(parents, kv, queries, upstream, part_dtype):
    rows, width = queries.shape
    blocks = rows // BLOCK
    pair_width = kv.shape[1]
    groups = width // (pair_width // 2)
    vmem = pl.BlockSpec(memory_space=pltpu.VMEM)
    return pl.pallas_call(
        attend,
        name="attend",
        out_shape=(
            jax.ShapeDtypeStruct(queries.shape, jnp.bfloat16),
            jax.ShapeDtypeStruct(queries.shape, jnp.bfloat16),
            jax.ShapeDtypeStruct(kv.shape, part_dtype),
        ),
        in_specs=[pl.BlockSpec(memory_space=pltpu.SMEM), vmem, vmem, vmem],
        out_specs=(vmem, vmem, vmem),
        scratch_shapes=[
            pltpu.VMEM((DEPTH // 2, 2 * BLOCK, groups * BLOCK), jnp.float32),
            pltpu.VMEM((blocks, DEPTH, BLOCK, pair_width), jnp.float32),
        ],
        compiler_params=pltpu.CompilerParams(vmem_limit_bytes=VMEM_LIMIT),
    )(parents, kv, queries, upstream)


def remote(src, dst, send_sem, recv_sem, ctx, tp):
    return pltpu.make_async_remote_copy(
        src_ref=src,
        dst_ref=dst,
        send_sem=send_sem,
        recv_sem=recv_sem,
        device_id=(ctx, tp),
        device_id_type=MESH,
    )


def greet(devices, count):
    barrier = pltpu.get_barrier_semaphore()
    for ctx, tp, valid in devices:
        if valid is None:
            pl.semaphore_signal(barrier, inc=1, device_id=(ctx, tp), device_id_type=MESH)
        else:

            @pl.when(valid)
            def _():
                pl.semaphore_signal(barrier, inc=1, device_id=(ctx, tp), device_id_type=MESH)

    pl.semaphore_wait(barrier, count)


class PlaneGather:
    def __init__(self, buf, chips, send, recv, sib_send, sib_recv):
        me, tp = lax.axis_index("ctx"), lax.axis_index("tp")
        self.buf, self.chips = buf, chips
        self.sems = (send, recv, sib_send, sib_recv)
        self.me, self.tp = me, tp
        self.chip, self.core = me // 2, me % 2

    def holder(self, offset):
        return (self.chip + self.chips - offset) % self.chips * 2

    def out_copy(self, offset):
        peer = (self.chip + offset) % self.chips * 2 + self.core
        slot = self.buf.at[self.me]
        return remote(
            slot, slot, self.sems[0].at[offset], self.sems[1].at[offset], peer, self.tp
        )

    def sib_copy(self, offset):
        slot = self.buf.at[self.holder(offset) + self.core]
        return remote(
            slot,
            slot,
            self.sems[2].at[offset],
            self.sems[3].at[offset],
            self.holder(0) + 1 - self.core,
            self.tp,
        )

    def start(self):
        for offset in range(1, self.chips):
            self.out_copy(offset).start()
        self.sib_copy(0).start()

    def arrive(self, offset):
        self.out_copy(offset).wait_recv()
        self.sib_copy(offset).start()
        return self.holder(offset) + self.core

    def arrive_sibling(self, offset):
        self.sib_copy(offset).wait_recv()
        return self.holder(offset) + 1 - self.core

    def drain(self):
        for offset in range(self.chips):
            if offset:
                self.out_copy(offset).wait_send()
            self.sib_copy(offset).wait_send()


class Line:
    def __init__(self, slot_of, size, sems):
        self.ctx, self.tp = lax.axis_index("ctx"), lax.axis_index("tp")
        self.slot_of, self.size, self.sems = slot_of, size, sems

    def send(self, way, k):
        source = self.tp - k if way == 0 else self.tp + k
        valid = (
            (source >= 0) & (self.tp < self.size - 1)
            if way == 0
            else (source < self.size) & (self.tp > 0)
        )
        slot = self.slot_of(source)
        target = self.tp + 1 if way == 0 else self.tp - 1
        return valid, remote(
            slot, slot, self.sems[0].at[way, k], self.sems[1].at[way, k], self.ctx, target
        )

    def start(self, k):
        for way in range(2):
            valid, copy = self.send(way, k)

            @pl.when(valid)
            def _(copy=copy):
                copy.start()

    def arrive(self, k, then):
        for way in range(2):
            source = self.tp - 1 - k if way == 0 else self.tp + 1 + k
            valid = source >= 0 if way == 0 else source < self.size
            slot = self.slot_of(source)

            @pl.when(valid)
            def _(way=way, source=source, slot=slot):
                remote(
                    slot, slot, self.sems[0].at[way, k], self.sems[1].at[way, k], self.ctx, self.tp
                ).wait_recv()
                if k + 1 < self.size - 1:
                    on, copy = self.send(way, k + 1)

                    @pl.when(on)
                    def _():
                        copy.start()

                then(way, source)

    def drain(self):
        for k in range(self.size - 1):
            for way in range(2):
                valid, copy = self.send(way, k)

                @pl.when(valid)
                def _(copy=copy):
                    copy.wait_send()


def gather_kernel(
    ctx_size,
    tp_size,
    merged,
    parents_ref,
    hid_ref,
    kw_ref,
    vw_ref,
    kw_any,
    vw_any,
    base_ref,
    near_ref,
    kv_ref,
    cols_ref,
    piece_ref,
    cos_ref,
    sin_ref,
    feat,
    acc,
    line_send,
    line_recv,
    kv_send,
    kv_recv,
    sib_send,
    sib_recv,
    col_send,
    col_recv,
    w_send,
    w_recv,
):
    me, tp = lax.axis_index("ctx"), lax.axis_index("tp")
    width, rows = hid_ref.shape
    half = width // 2
    key_width = kw_ref.shape[1]
    blocks = rows // BLOCK
    col_rows = cols_ref.shape[1]
    per_half = half // col_rows
    greet(
        [((me + o) % ctx_size, tp, None) for o in range(1, ctx_size)]
        + [(me, (tp + o) % tp_size, None) for o in range(1, tp_size)],
        ctx_size + tp_size - 2,
    )
    for j in range(2):
        feat[tp, j] = hid_ref[j * half : (j + 1) * half, :]
    lines = [
        Line(lambda s, j=j: feat.at[s, j], tp_size, (line_send.at[j], line_recv.at[j]))
        for j in range(2)
    ]
    lines[0].start(0)

    def col_copy(source, j, i):
        dest = (source * 2 + j) * per_half + i
        offset = (dest + ctx_size - me) % ctx_size
        return dest, remote(
            feat.at[source, j, pl.ds(i * col_rows, col_rows), :],
            cols_ref.at[me],
            col_send.at[offset],
            col_recv.at[offset],
            dest,
            tp,
        )

    def share(source, j):
        for i in range(per_half):
            dest, copy = col_copy(source, j, i)

            @pl.when(dest != me)
            def _(copy=copy):
                copy.start()

            @pl.when(dest == me)
            def _(i=i):
                cols_ref[me] = feat[source, j, i * col_rows : (i + 1) * col_rows, :]

    def project(source, j):
        at = pl.ds(pl.multiple_of(source * width + j * half, 128), half)
        block = feat[source, j]
        acc[:, :key_width] += dot_f32(block, kw_ref[at, :], 0, 0)
        acc[:, key_width:] += dot_f32(block, vw_ref[at, :], 0, 0)

    acc[...] = jnp.zeros_like(acc)
    lines[1].start(0)
    for j in range(2):
        share(tp, j)

    first = me * blocks
    lane = lax.broadcasted_iota(jnp.int32, (BLOCK, HD), 1)
    sign = jnp.where(lane < HD // 2, -1.0, 1.0)
    for b in range(blocks):
        depth, _ = walk(parents_ref, first + b)
        pick = lax.broadcasted_iota(jnp.int32, (DEPTH, HD), 0) == depth
        base_cos = jnp.sum(jnp.where(pick, base_ref[0], 0.0), axis=0, keepdims=True)
        base_sin = jnp.sum(jnp.where(pick, base_ref[1], 0.0), axis=0, keepdims=True)
        at = slice(b * BLOCK, (b + 1) * BLOCK)
        cos_ref[at, :] = base_cos * near_ref[0] - base_sin * near_ref[1]
        sin_ref[at, :] = (base_sin * near_ref[0] + base_cos * near_ref[1]) * sign

    for j in range(2):
        project(tp, j)
    late = []
    for j in range(2):
        for k in range(tp_size - 1):
            last = j == 1 and k == tp_size - 2

            def then(way, source, j=j, last=last):
                if not last:
                    share(source, j)
                project(source, j)

            lines[j].arrive(k, then)

    def piece_copy(offset, matrix):
        target = (tp + offset) % tp_size
        return remote(
            (kw_any, vw_any)[matrix].at[target, me],
            piece_ref.at[tp_size - 1 - offset, matrix],
            w_send.at[offset, matrix],
            w_recv.at[offset, matrix],
            me,
            target,
        )

    for offset in range(1, tp_size):
        for matrix in range(2):
            piece_copy(offset, matrix).start()

    cosine, sine = cos_ref[...], sin_ref[...]
    for g in range(key_width // HD):
        at = slice(g * HD, (g + 1) * HD)
        x = acc[:, at]
        kv_ref[me, :, at] = (x * cosine + pltpu.roll(x, HD // 2, 1) * sine).astype(jnp.bfloat16)
    kv_ref[me, :, key_width:] = acc[:, key_width:].astype(jnp.bfloat16)
    gather = PlaneGather(kv_ref, ctx_size // 2, kv_send, kv_recv, sib_send, sib_recv)
    gather.start()
    for offset in range(1, ctx_size // 2):
        gather.arrive(offset)
    k = tp_size - 2
    for way in range(2):
        source = tp - 1 - k if way == 0 else tp + 1 + k
        valid = source >= 0 if way == 0 else source < tp_size

        @pl.when(valid)
        def _(source=source):
            share(source, 1)

    for offset in range(ctx_size // 2):
        gather.arrive_sibling(offset)
    if merged is not None:
        merged()
    for offset in range(1, ctx_size):
        remote(
            cols_ref.at[(me + ctx_size - offset) % ctx_size],
            cols_ref.at[(me + ctx_size - offset) % ctx_size],
            col_send.at[offset],
            col_recv.at[offset],
            me,
            tp,
        ).wait()
    for offset in range(1, tp_size):
        for matrix in range(2):
            piece_copy(offset, matrix).wait()
    gather.drain()
    for line in lines:
        line.drain()


def grads_kernel(
    ctx_size,
    tp_size,
    part_ref,
    cos_ref,
    sin_ref,
    cols_ref,
    piece_ref,
    kw_ref,
    vw_ref,
    hg_ref,
    kwg_ref,
    vwg_ref,
    total,
    sib_buf,
    chip_buf,
    rs_buf,
    gbuf,
    zbuf,
    wall,
    hg_acc,
    a_send,
    a_recv,
    b_send,
    b_recv,
    g_send,
    g_recv,
    gs_send,
    gs_recv,
    w_send,
    w_recv,
    ws_send,
    ws_recv,
    line_send,
    line_recv,
):
    me, tp = lax.axis_index("ctx"), lax.axis_index("tp")
    chips = ctx_size // 2
    chip, core = me // 2, me % 2
    rows, pair_width = total.shape
    key_width = pair_width // 2
    up, down = tp < tp_size - 1, tp > 0
    sibling = chip * 2 + 1 - core
    greet(
        [((chip + o) % chips * 2 + core, tp, None) for o in range(1, chips)]
        + [(sibling, tp, None)]
        + [(me, jnp.minimum(tp + 1, tp_size - 1), up), (me, jnp.maximum(tp - 1, 0), down)],
        chips + jnp.where(up, 1, 0) + jnp.where(down, 1, 0),
    )

    def sib_copy(offset):
        target = (chip + offset) % chips
        return remote(
            part_ref.at[target * 2 + 1 - core],
            sib_buf.at[offset],
            a_send.at[offset],
            a_recv.at[offset],
            sibling,
            tp,
        )

    def chip_copy(offset):
        target = (chip + offset) % chips
        return remote(
            chip_buf.at[offset],
            rs_buf.at[offset],
            b_send.at[offset],
            b_recv.at[offset],
            target * 2 + core,
            tp,
        )

    order = list(range(1, chips)) + [0]
    for offset in order:
        sib_copy(offset).start()
    wall[me] = piece_ref[...]
    for offset in order:
        sib_copy(offset).wait_recv()
        own = part_ref[(chip + offset) % chips * 2 + core]
        both = own.astype(jnp.float32) + sib_buf[offset].astype(jnp.float32)
        if offset:
            chip_buf[offset] = both.astype(jnp.bfloat16)
            chip_copy(offset).start()
        else:
            total[...] = both
    weights = PlaneGather(wall, chips, w_send, w_recv, ws_send, ws_recv)
    for offset in range(1, chips):
        chip_copy(offset).wait_recv()
        total[...] += rs_buf[offset].astype(jnp.float32)
    cosine, sine = cos_ref[...], sin_ref[...]
    for g in range(key_width // HD):
        at = slice(g * HD, (g + 1) * HD)
        x = total[:, at]
        zbuf[tp, :, at] = (x * cosine - pltpu.roll(x, HD // 2, 1) * sine).astype(jnp.bfloat16)
    zbuf[tp, :, key_width:] = total[:, key_width:].astype(jnp.bfloat16)
    gbuf[me] = zbuf[tp]
    line = Line(lambda s: zbuf.at[s], tp_size, (line_send, line_recv))
    line.start(0)
    grads = PlaneGather(gbuf, chips, g_send, g_recv, gs_send, gs_recv)
    grads.start()
    weights.start()

    def weight_grad(source, fresh=False):
        left = cols_ref[source]
        key_part = dot_f32(left, gbuf[source, :, :key_width], 1, 0)
        value_part = dot_f32(left, gbuf[source, :, key_width:], 1, 0)
        if fresh:
            kwg_ref[...] = key_part
            vwg_ref[...] = value_part
        else:
            kwg_ref[...] += key_part
            vwg_ref[...] += value_part

    def hidden_grad(source, key_rows, value_rows):
        part = dot_f32(zbuf[source, :, :key_width], key_rows, 1, 1) + dot_f32(
            zbuf[source, :, key_width:], value_rows, 1, 1
        )
        return part.astype(jnp.bfloat16).astype(jnp.float32)

    weight_grad(me, True)
    hg_acc[...] = hidden_grad(tp, kw_ref[...], vw_ref[...])
    line.arrive(0, lambda way, source: None)
    for offset in range(1, chips):
        weight_grad(grads.arrive(offset))
        if offset < tp_size - 1:
            line.arrive(offset, lambda way, source: None)
    for k in range(chips, tp_size - 1):
        line.arrive(k, lambda way, source: None)
    for offset in range(1, chips):
        weights.arrive(offset)
    for offset in range(chips):
        weight_grad(grads.arrive_sibling(offset))
    for offset in range(chips):
        weights.arrive_sibling(offset)

    def rows_of(j, matrix):
        pieces = [wall[c, j, matrix] for c in range(ctx_size)]
        if wall.shape[3] % 16:
            pieces = [piece.astype(jnp.float32) for piece in pieces]
        return jnp.concatenate(pieces, axis=0).astype(jnp.bfloat16)

    for j in range(tp_size - 1):
        source = (tp + 1 + j) % tp_size
        hg_acc[...] += hidden_grad(source, rows_of(j, 0), rows_of(j, 1))
    hg_ref[...] = hg_acc[...].astype(jnp.bfloat16)
    for offset in range(chips):
        sib_copy(offset).wait_send()
        if offset:
            chip_copy(offset).wait_send()
    grads.drain()
    weights.drain()
    line.drain()


def rope_tables():
    lane = jnp.arange(HD, dtype=jnp.int32) % (HD // 2)
    frequency = jnp.exp(lane.astype(jnp.float32) * (-2.0 * math.log(THETA) / HD))
    base = (jnp.arange(DEPTH, dtype=jnp.int32) * BLOCK).astype(jnp.float32)[:, None] * frequency
    near = jnp.arange(BLOCK, dtype=jnp.int32).astype(jnp.float32)[:, None] * frequency
    return (
        jnp.stack([jnp.cos(base), jnp.sin(base)]),
        jnp.stack([jnp.cos(near), jnp.sin(near)]),
    )


def shards(ctx_size, tp_size, hidden, queries, key_weight, value_weight, parents, upstream):
    rows, width = hidden.shape
    depth_rows, key_width = key_weight.shape
    pair_width = 2 * key_width
    col_rows = depth_rows // ctx_size
    piece_rows = width // ctx_size
    chips = ctx_size // 2
    vmem = pl.BlockSpec(memory_space=pltpu.VMEM)
    anywhere = pl.BlockSpec(memory_space=pl.ANY)
    smem = pl.BlockSpec(memory_space=pltpu.SMEM)
    bf16, f32 = jnp.bfloat16, jnp.float32
    dma = pltpu.SemaphoreType.DMA
    base, near = rope_tables()
    split = (tp_size, ctx_size, piece_rows, key_width)

    def params(collective_id):
        return pltpu.CompilerParams(
            collective_id=collective_id, has_side_effects=True, vmem_limit_bytes=VMEM_LIMIT
        )

    kv, cols, pieces, cosine, sine = pl.pallas_call(
        partial(gather_kernel, ctx_size, tp_size, None),
        name="gather_keys_values",
        out_shape=(
            jax.ShapeDtypeStruct((ctx_size, rows, pair_width), bf16),
            jax.ShapeDtypeStruct((ctx_size, col_rows, rows), bf16),
            jax.ShapeDtypeStruct((tp_size - 1, 2, piece_rows, key_width), bf16),
            jax.ShapeDtypeStruct((rows, HD), f32),
            jax.ShapeDtypeStruct((rows, HD), f32),
        ),
        in_specs=[smem, vmem, vmem, vmem, anywhere, anywhere, vmem, vmem],
        out_specs=(vmem,) * 5,
        scratch_shapes=[
            pltpu.VMEM((tp_size, 2, width // 2, rows), bf16),
            pltpu.VMEM((rows, pair_width), f32),
            dma((2, 2, tp_size - 1)),
            dma((2, 2, tp_size - 1)),
            dma((chips,)),
            dma((chips,)),
            dma((chips,)),
            dma((chips,)),
            dma((ctx_size,)),
            dma((ctx_size,)),
            dma((tp_size, 2)),
            dma((tp_size, 2)),
        ],
        compiler_params=params(1),
    )(
        parents,
        hidden.T,
        key_weight,
        value_weight,
        key_weight.reshape(split),
        value_weight.reshape(split),
        base,
        near,
    )
    attention, query_grad, part = attention_call(
        parents, kv.reshape(ctx_size * rows, pair_width), queries, upstream, bf16
    )
    first = lax.axis_index("tp") * width
    kw_own = lax.dynamic_slice_in_dim(key_weight, first, width, 0)
    vw_own = lax.dynamic_slice_in_dim(value_weight, first, width, 0)
    hidden_grad, key_weight_grad, value_weight_grad = pl.pallas_call(
        partial(grads_kernel, ctx_size, tp_size),
        name="sum_grads",
        out_shape=(
            jax.ShapeDtypeStruct(hidden.shape, bf16),
            jax.ShapeDtypeStruct((col_rows, key_width), f32),
            jax.ShapeDtypeStruct((col_rows, key_width), f32),
        ),
        in_specs=[vmem] * 7,
        out_specs=(vmem,) * 3,
        scratch_shapes=[
            pltpu.VMEM((rows, pair_width), f32),
            pltpu.VMEM((chips, rows, pair_width), bf16),
            pltpu.VMEM((chips, rows, pair_width), bf16),
            pltpu.VMEM((chips, rows, pair_width), bf16),
            pltpu.VMEM((ctx_size, rows, pair_width), bf16),
            pltpu.VMEM((tp_size, rows, pair_width), bf16),
            pltpu.VMEM((ctx_size, tp_size - 1, 2, piece_rows, key_width), bf16),
            pltpu.VMEM((rows, width), f32),
        ]
        + [dma((chips,))] * 12
        + [dma((2, tp_size - 1))] * 2,
        compiler_params=params(2),
    )(
        part.reshape(ctx_size, rows, pair_width),
        cosine,
        sine,
        cols,
        pieces,
        kw_own,
        vw_own,
    )
    return attention, query_grad, hidden_grad, key_weight_grad, value_weight_grad


def solution(mesh):
    return jax.shard_map(
        partial(shards, mesh.shape["ctx"], mesh.shape["tp"]),
        mesh=mesh,
        in_specs=(
            P("ctx", "tp"),
            P("ctx", "tp"),
            P(None, "tp"),
            P(None, "tp"),
            P(),
            P("ctx", "tp"),
        ),
        out_specs=(P("ctx", "tp"),) * 5,
        check_vma=False,
    )
```

```python
from functools import partial
import math

import jax
import jax.numpy as jnp
from jax import lax
from jax.experimental import pallas as pl
from jax.experimental.pallas import tpu as pltpu
from jax.sharding import PartitionSpec as P

HD = 128
BLOCK = 128
DEPTH = 8
THETA = 1000000.0
NEGATIVE = -1e30
VMEM_LIMIT = 56 * 1024 * 1024
MESH = pl.DeviceIdType.MESH


def walk(parents_ref, block):
    chain = [block]
    for _ in range(DEPTH - 1):
        last = chain[-1]
        above = parents_ref[jnp.maximum(last, 0)]
        chain.append(jnp.where(last > 0, above, -1))
    depth = jnp.int32(0)
    for node in chain[1:]:
        depth = depth + jnp.where(node >= 0, 1, 0)
    path = []
    for level in range(DEPTH):
        found = jnp.int32(0)
        for hop in range(DEPTH):
            found = found + jnp.where(depth - hop == level, chain[hop], 0)
        path.append(found)
    return depth, path


def dot_f32(left, right, left_dim, right_dim):
    return lax.dot_general(
        left, right, (((left_dim,), (right_dim,)), ((), ())), preferred_element_type=jnp.float32
    )


def attend(parents_ref, kv_ref, q_ref, u_ref, att_ref, qg_ref, s_ref, grads_ref, release):
    rows, width = q_ref.shape
    blocks = rows // BLOCK
    pair_width = kv_ref.shape[2]
    key_width = pair_width // 2
    key_heads = key_width // HD
    groups = width // key_width
    lanes = groups * BLOCK
    step = 2 * BLOCK
    steps = DEPTH // 2
    scale = 1.0 / math.sqrt(HD)
    first = lax.axis_index("ctx") * blocks

    def one_block(b, carry):
        depth, path = walk(parents_ref, first + b)
        row0 = pl.multiple_of(b * BLOCK, BLOCK)
        here = pl.ds(row0, BLOCK)
        key_row = lax.broadcasted_iota(jnp.int32, (step, lanes), 0)
        query_row = lax.broadcasted_iota(jnp.int32, (step, lanes), 1) % BLOCK
        limit = depth * BLOCK + query_row - key_row
        for g in range(key_heads):
            def head_cols(h):
                return slice((g * groups + h) * HD, (g * groups + h + 1) * HD)

            key_cols = slice(g * HD, (g + 1) * HD)
            value_cols = slice(key_width + g * HD, key_width + (g + 1) * HD)
            q = jnp.concatenate([q_ref[here, head_cols(h)] for h in range(groups)], axis=0)
            u = jnp.concatenate([u_ref[here, head_cols(h)] for h in range(groups)], axis=0)
            u_t = u.astype(jnp.float32).T

            def pair(p, cols):
                return jnp.concatenate(
                    [
                        kv_ref[path[2 * p + i], :, cols] for i in range(2)
                    ],
                    axis=0,
                )

            top = jnp.full((1, lanes), NEGATIVE, jnp.float32)
            for p in range(steps):
                s = dot_f32(pair(p, key_cols), q, 1, 1) * scale
                s = jnp.where(limit >= p * step, s, NEGATIVE)
                s_ref[p] = s
                top = jnp.maximum(top, jnp.max(s, axis=0, keepdims=True))
            totals = jnp.zeros((1, lanes), jnp.float32)
            mixed = jnp.zeros((HD, lanes), jnp.float32)
            for p in range(steps):
                w = jnp.exp(s_ref[p] - top)
                s_ref[p] = w
                totals = totals + jnp.sum(w, axis=0, keepdims=True)
                mixed = mixed + dot_f32(pair(p, value_cols), w.astype(jnp.bfloat16), 0, 0)
            out_t = (mixed / totals).astype(jnp.bfloat16).astype(jnp.float32)
            out = out_t.T.astype(jnp.bfloat16)
            for h in range(groups):
                att_ref[here, head_cols(h)] = out[h * BLOCK : (h + 1) * BLOCK]
            deltas = jnp.sum(out_t * u_t, axis=0, keepdims=True)
            inverse = 1.0 / totals
            query_grad = jnp.zeros((HD, lanes), jnp.float32)
            for p in range(steps):
                prob = s_ref[p] * inverse
                value_part = dot_f32(prob.astype(jnp.bfloat16), u, 1, 0)
                prob_grad = dot_f32(pair(p, value_cols), u, 1, 1)
                ds = (prob * (prob_grad - deltas)).astype(jnp.bfloat16)
                key_part = dot_f32(ds, q, 1, 0) * scale
                query_grad = query_grad + dot_f32(pair(p, key_cols), ds, 0, 0)
                for i in range(2):
                    grads_ref[b, 2 * p + i, :, key_cols] = key_part[i * BLOCK : (i + 1) * BLOCK]
                    grads_ref[b, 2 * p + i, :, value_cols] = value_part[i * BLOCK : (i + 1) * BLOCK]
            qg = (query_grad * scale).T.astype(jnp.bfloat16)
            for h in range(groups):
                qg_ref[here, head_cols(h)] = qg[h * BLOCK : (h + 1) * BLOCK]
        return carry

    lax.fori_loop(0, blocks, one_block, 0)

    release()
    part_ref = kv_ref
    paths = [walk(parents_ref, first + b) for b in range(blocks)]
    block_total = part_ref.shape[0]

    def one_target(target, carry):
        total = jnp.zeros((BLOCK, pair_width), jnp.float32)
        for b in range(blocks):
            depth, path = paths[b]
            slot = jnp.int32(0)
            hits = jnp.int32(0)
            for level in range(DEPTH):
                hit = jnp.where((path[level] == target) & (depth >= level), 1, 0)
                slot = slot + hit * level
                hits = hits + hit
            total = total + grads_ref[b, slot] * hits.astype(jnp.float32)
        part_ref[target] = total.astype(part_ref.dtype)
        return carry

    lax.fori_loop(0, block_total, one_target, 0)


def remote(src, dst, send_sem, recv_sem, ctx, tp):
    return pltpu.make_async_remote_copy(
        src_ref=src,
        dst_ref=dst,
        send_sem=send_sem,
        recv_sem=recv_sem,
        device_id=(ctx, tp),
        device_id_type=MESH,
    )


def greet(devices, count):
    barrier = pltpu.get_barrier_semaphore()
    for ctx, tp, valid in devices:
        if valid is None:
            pl.semaphore_signal(barrier, inc=1, device_id=(ctx, tp), device_id_type=MESH)
        else:

            @pl.when(valid)
            def _():
                pl.semaphore_signal(barrier, inc=1, device_id=(ctx, tp), device_id_type=MESH)

    pl.semaphore_wait(barrier, count)


class PlaneGather:
    def __init__(self, buf, span, chips, relay, sems):
        me, tp = lax.axis_index("ctx"), lax.axis_index("tp")
        self.buf, self.span = buf, span
        self.chips, self.relay = chips, relay and chips == 4
        self.sems = sems
        self.me, self.tp = me, tp
        self.chip, self.core = me // 2, me % 2

    def slot(self, index):
        return self.buf.at[pl.ds(index * self.span, self.span)]

    def holder(self, offset):
        if self.relay:
            along_x = self.chip + (1 - 2 * (self.chip % 2) if offset % 2 else 0)
            return (along_x + (2 if offset >= 2 else 0)) % 4 * 2
        return (self.chip + self.chips - offset) % self.chips * 2

    def out_copy(self, offset):
        peer = (self.chip + offset) % self.chips * 2
        slot = self.slot(self.me)
        if self.relay:
            peer = self.holder(offset)
            if offset == 3:
                one, two = self.holder(1), self.holder(2)
                peer = two * (1 - self.core) + one * self.core
                slot = self.slot(one * (1 - self.core) + two * self.core + self.core)
        return remote(
            slot,
            slot,
            self.sems[0].at[offset],
            self.sems[1].at[offset],
            peer + self.core,
            self.tp,
        )

    def sib_copy(self, offset):
        slot = self.slot(self.holder(offset) + self.core)
        return remote(
            slot,
            slot,
            self.sems[2].at[offset],
            self.sems[3].at[offset],
            self.holder(0) + 1 - self.core,
            self.tp,
        )

    def start(self):
        for offset in range(1, 3 if self.relay else self.chips):
            self.out_copy(offset).start()
        self.sib_copy(0).start()

    def arrive(self, offset):
        self.out_copy(offset).wait_recv()
        if self.relay and offset < 3:

            @pl.when(self.core == offset - 1)
            def _():
                self.out_copy(3).start()

        self.sib_copy(offset).start()
        return self.holder(offset) + self.core

    def arrive_sibling(self, offset):
        self.sib_copy(offset).wait_recv()
        return self.holder(offset) + 1 - self.core

    def drain(self):
        for offset in range(self.chips):
            if offset:
                self.out_copy(offset).wait_send()
            self.sib_copy(offset).wait_send()


class Line:
    def __init__(self, slot_of, size, sems):
        self.ctx, self.tp = lax.axis_index("ctx"), lax.axis_index("tp")
        self.slot_of, self.size, self.sems = slot_of, size, sems

    def send(self, way, k):
        source = self.tp - k if way == 0 else self.tp + k
        valid = (
            (source >= 0) & (self.tp < self.size - 1)
            if way == 0
            else (source < self.size) & (self.tp > 0)
        )
        slot = self.slot_of(source)
        target = self.tp + 1 if way == 0 else self.tp - 1
        return valid, remote(
            slot, slot, self.sems[0].at[way, k], self.sems[1].at[way, k], self.ctx, target
        )

    def start(self, k):
        for way in range(2):
            valid, copy = self.send(way, k)

            @pl.when(valid)
            def _(copy=copy):
                copy.start()

    def arrive(self, k, then):
        for way in range(2):
            source = self.tp - 1 - k if way == 0 else self.tp + 1 + k
            valid = source >= 0 if way == 0 else source < self.size
            slot = self.slot_of(source)

            @pl.when(valid)
            def _(way=way, source=source, slot=slot):
                remote(
                    slot, slot, self.sems[0].at[way, k], self.sems[1].at[way, k], self.ctx, self.tp
                ).wait_recv()
                if k + 1 < self.size - 1:
                    on, copy = self.send(way, k + 1)

                    @pl.when(on)
                    def _():
                        copy.start()

                then(way, source)

    def drain(self):
        for k in range(self.size - 1):
            for way in range(2):
                valid, copy = self.send(way, k)

                @pl.when(valid)
                def _(copy=copy):
                    copy.wait_send()


def sum_grads(
    ctx_size,
    tp_size,
    part_ref,
    cos_ref,
    sin_ref,
    kw_ref,
    vw_ref,
    cols_ref,
    wall,
    weights,
    hg_ref,
    kwg_ref,
    vwg_ref,
    total,
    sib_buf,
    rs_buf,
    gbuf,
    zbuf,
    hg_acc,
    a_sems,
    b_sems,
    g_sems,
    z_sems,
    wait_columns,
):
    me, tp = lax.axis_index("ctx"), lax.axis_index("tp")
    chips = ctx_size // 2
    chip, core = me // 2, me % 2
    rows, pair_width = total.shape
    blocks = sib_buf.shape[1]
    width = hg_ref.shape[1]
    strip = hg_acc.shape[2]
    key_width = pair_width // 2
    sibling = chip * 2 + 1 - core

    def sib_copy(offset):
        target = (chip + offset) % chips
        return remote(
            part_ref.at[pl.ds((target * 2 + 1 - core) * blocks, blocks)],
            sib_buf.at[offset],
            a_sems[0].at[offset],
            a_sems[1].at[offset],
            sibling,
            tp,
        )

    def chip_copy(offset):
        target = (chip + offset) % chips
        return remote(
            sib_buf.at[offset],
            rs_buf.at[offset - 1],
            b_sems[0].at[offset],
            b_sems[1].at[offset],
            target * 2 + core,
            tp,
        )

    order = list(range(1, chips)) + [0]
    for offset in order:
        sib_copy(offset).start()
    for offset in order:
        sib_copy(offset).wait_recv()
        own = part_ref[pl.ds(((chip + offset) % chips * 2 + core) * blocks, blocks)]
        both = own.astype(jnp.float32) + sib_buf[offset].astype(jnp.float32)
        if offset:
            sib_buf[offset] = both.astype(jnp.bfloat16)
            chip_copy(offset).start()
        else:
            total[...] = both.reshape(total.shape)
    for offset in range(1, chips):
        chip_copy(offset).wait_recv()
        total[...] += rs_buf[offset - 1].astype(jnp.float32).reshape(total.shape)
    cosine, sine = cos_ref[...], sin_ref[...]
    for g in range(key_width // HD):
        at = slice(g * HD, (g + 1) * HD)
        x = total[:, at]
        zbuf[tp, :, at] = (x * cosine - pltpu.roll(x, HD // 2, 1) * sine).astype(jnp.bfloat16)
    zbuf[tp, :, key_width:] = total[:, key_width:].astype(jnp.bfloat16)
    gbuf[me] = zbuf[tp]
    line = Line(lambda s: zbuf.at[s], tp_size, z_sems)
    line.start(0)
    grads = PlaneGather(gbuf, 1, chips, True, g_sems)
    grads.start()

    def weight_grad(source, fresh=False):
        left = cols_ref[source]
        key_part = dot_f32(left, gbuf[source, :, :key_width], 1, 0)
        value_part = dot_f32(left, gbuf[source, :, key_width:], 1, 0)
        if fresh:
            kwg_ref[...] = key_part
            vwg_ref[...] = value_part
        else:
            kwg_ref[...] += key_part
            vwg_ref[...] += value_part

    def hidden_grad(source, key_rows, value_rows, fresh=False):
        for n in range(width // strip):
            at = slice(n * strip, (n + 1) * strip)
            part = dot_f32(zbuf[source, :, :key_width], key_rows[at], 1, 1) + dot_f32(
                zbuf[source, :, key_width:], value_rows[at], 1, 1
            )
            part = part.astype(jnp.bfloat16).astype(jnp.float32)
            hg_acc[n] = part if fresh else hg_acc[n] + part

    own = pl.ds(pl.multiple_of(tp * width, 128), width)
    for offset in range(1, ctx_size):
        wait_columns(offset)
    weight_grad(me, True)
    hidden_grad(tp, kw_ref[own, :], vw_ref[own, :], True)
    line.arrive(0, lambda way, source: None)
    for offset in range(1, chips):
        weights.arrive(offset)
    for offset in range(1, chips):
        weight_grad(grads.arrive(offset))
        if offset < tp_size - 1:
            line.arrive(offset, lambda way, source: None)
    for k in range(chips, tp_size - 1):
        line.arrive(k, lambda way, source: None)
    for offset in range(chips):
        weight_grad(grads.arrive_sibling(offset))
    for offset in range(chips):
        weights.arrive_sibling(offset)

    def rows_of(j, matrix):
        pieces = [wall[c, j, matrix] for c in range(ctx_size)]
        if wall.shape[3] % 16:
            pieces = [piece.astype(jnp.float32) for piece in pieces]
        return jnp.concatenate(pieces, axis=0).astype(jnp.bfloat16)

    for j in range(tp_size - 1):
        source = (tp + 1 + j) % tp_size
        hidden_grad(source, rows_of(j, 0), rows_of(j, 1))
    for n in range(width // strip):
        hg_ref[:, n * strip : (n + 1) * strip] = hg_acc[n].astype(jnp.bfloat16)
    for offset in range(chips):
        sib_copy(offset).wait_send()
        if offset:
            chip_copy(offset).wait_send()
    grads.drain()
    weights.drain()
    line.drain()


def layer_kernel(
    ctx_size,
    tp_size,
    parents_ref,
    hid_ref,
    kw_hbm,
    vw_hbm,
    kw_any,
    vw_any,
    q_hbm,
    u_hbm,
    base_ref,
    near_ref,
    att_ref,
    qg_ref,
    hg_ref,
    kwg_ref,
    vwg_ref,
    feat,
    acc,
    kw_ref,
    vw_ref,
    q_ref,
    u_ref,
    kv_ref,
    cols_ref,
    cos_ref,
    sin_ref,
    wall,
    s_ref,
    slot_ref,
    sib_buf,
    rs_buf,
    gbuf,
    zbuf,
    load_sem,
    line_send,
    line_recv,
    col_send,
    col_recv,
    w_send,
    w_recv,
    kv_sems_0,
    kv_sems_1,
    kv_sems_2,
    kv_sems_3,
    wall_sems_0,
    wall_sems_1,
    wall_sems_2,
    wall_sems_3,
    a_sems_0,
    a_sems_1,
    b_sems_0,
    b_sems_1,
    g_sems_0,
    g_sems_1,
    g_sems_2,
    g_sems_3,
    z_send,
    z_recv,
):
    kv_sems = (kv_sems_0, kv_sems_1, kv_sems_2, kv_sems_3)
    wall_sems = (wall_sems_0, wall_sems_1, wall_sems_2, wall_sems_3)
    a_sems = (a_sems_0, a_sems_1)
    b_sems = (b_sems_0, b_sems_1)
    g_sems = (g_sems_0, g_sems_1, g_sems_2, g_sems_3)
    z_sems = (z_send, z_recv)
    me, tp = lax.axis_index("ctx"), lax.axis_index("tp")
    width, rows = hid_ref.shape
    loads = [
        pltpu.make_async_copy(source, held, load_sem.at[i])
        for i, (source, held) in enumerate(
            [(kw_hbm, kw_ref), (vw_hbm, vw_ref), (q_hbm, q_ref), (u_hbm, u_ref)]
        )
    ]
    for load in loads:
        load.start()
    half = width // 2
    key_width = kw_ref.shape[1]
    blocks = rows // BLOCK
    chips = ctx_size // 2
    col_rows = cols_ref.shape[1]
    per_half = half // col_rows
    greet(
        [((me + o) % ctx_size, tp, None) for o in range(1, ctx_size)]
        + [(me, (tp + o) % tp_size, None) for o in range(1, tp_size)],
        ctx_size + tp_size - 2,
    )
    for j in range(2):
        feat[tp, j] = hid_ref[j * half : (j + 1) * half, :]
    lines = [
        Line(lambda s, j=j: feat.at[s, j], tp_size, (line_send.at[j], line_recv.at[j]))
        for j in range(2)
    ]
    lines[0].start(0)

    def col_copy(source, j, i):
        dest = (source * 2 + j) * per_half + i
        offset = (dest + ctx_size - me) % ctx_size
        return dest, remote(
            feat.at[source, j, pl.ds(i * col_rows, col_rows), :],
            cols_ref.at[me],
            col_send.at[offset],
            col_recv.at[offset],
            dest,
            tp,
        )

    def share(source, j):
        for i in range(per_half):
            dest, copy = col_copy(source, j, i)

            @pl.when(dest != me)
            def _(copy=copy):
                copy.start()

            @pl.when(dest == me)
            def _(i=i):
                cols_ref[me] = feat[source, j, i * col_rows : (i + 1) * col_rows, :]

    def project(source, j):
        at = pl.ds(pl.multiple_of(source * width + j * half, 128), half)
        block = feat[source, j]
        acc[:, :key_width] += dot_f32(block, kw_ref[at, :], 0, 0)
        acc[:, key_width:] += dot_f32(block, vw_ref[at, :], 0, 0)

    def wait_columns(offset):
        source = (me + ctx_size - offset) % ctx_size
        slot = cols_ref.at[source]
        remote(slot, slot, col_send.at[offset], col_recv.at[offset], me, tp).wait()

    acc[...] = jnp.zeros_like(acc)
    lines[1].start(0)
    for j in range(2):
        share(tp, j)

    first = me * blocks
    lane = lax.broadcasted_iota(jnp.int32, (BLOCK, HD), 1)
    sign = jnp.where(lane < HD // 2, -1.0, 1.0)
    for b in range(blocks):
        depth, _ = walk(parents_ref, first + b)
        pick = lax.broadcasted_iota(jnp.int32, (DEPTH, HD), 0) == depth
        base_cos = jnp.sum(jnp.where(pick, base_ref[0], 0.0), axis=0, keepdims=True)
        base_sin = jnp.sum(jnp.where(pick, base_ref[1], 0.0), axis=0, keepdims=True)
        at = slice(b * BLOCK, (b + 1) * BLOCK)
        cos_ref[at, :] = base_cos * near_ref[0] - base_sin * near_ref[1]
        sin_ref[at, :] = (base_sin * near_ref[0] + base_cos * near_ref[1]) * sign

    for load in loads[:2]:
        load.wait()
    for j in range(2):
        project(tp, j)
    for j in range(2):
        for k in range(tp_size - 1):
            last = j == 1 and k == tp_size - 2

            def then(way, source, j=j, last=last):
                if not last:
                    share(source, j)
                project(source, j)

            lines[j].arrive(k, then)

    def piece_copy(offset, matrix):
        target = (tp + offset) % tp_size
        return remote(
            (kw_any, vw_any)[matrix].at[target, me],
            wall.at[me, tp_size - 1 - offset, matrix],
            w_send.at[offset, matrix],
            w_recv.at[offset, matrix],
            me,
            target,
        )

    for line in lines:
        line.drain()
    for offset in range(1, tp_size):
        for matrix in range(2):
            piece_copy(offset, matrix).start()

    cosine, sine = cos_ref[...], sin_ref[...]
    for g in range(key_width // HD):
        at = slice(g * HD, (g + 1) * HD)
        x = acc[:, at]
        keys = (x * cosine + pltpu.roll(x, HD // 2, 1) * sine).astype(jnp.bfloat16)
        for b in range(blocks):
            kv_ref[first + b, :, at] = keys[b * BLOCK : (b + 1) * BLOCK]
    for b in range(blocks):
        kv_ref[first + b, :, key_width:] = acc[
            b * BLOCK : (b + 1) * BLOCK, key_width:
        ].astype(jnp.bfloat16)
    gather = PlaneGather(kv_ref, blocks, chips, True, kv_sems)
    gather.start()
    for offset in range(1, chips):
        gather.arrive(offset)
    k = tp_size - 2
    for way in range(2):
        source = tp - 1 - k if way == 0 else tp + 1 + k
        valid = source >= 0 if way == 0 else source < tp_size

        @pl.when(valid)
        def _(source=source):
            share(source, 1)

    for offset in range(chips):
        gather.arrive_sibling(offset)
    for offset in range(1, tp_size):
        for matrix in range(2):
            piece_copy(offset, matrix).wait()
    weights = PlaneGather(wall, 1, chips, False, wall_sems)
    weights.start()
    for load in loads[2:]:
        load.wait()
    attend(parents_ref, kv_ref, q_ref, u_ref, att_ref, qg_ref, s_ref, slot_ref, gather.drain)
    sum_grads(
        ctx_size,
        tp_size,
        kv_ref,
        cos_ref,
        sin_ref,
        kw_ref,
        vw_ref,
        cols_ref,
        wall,
        weights,
        hg_ref,
        kwg_ref,
        vwg_ref,
        acc,
        sib_buf,
        rs_buf,
        gbuf,
        zbuf,
        s_ref,
        a_sems,
        b_sems,
        g_sems,
        z_sems,
        wait_columns,
    )


def rope_tables():
    lane = jnp.arange(HD, dtype=jnp.int32) % (HD // 2)
    frequency = jnp.exp(lane.astype(jnp.float32) * (-2.0 * math.log(THETA) / HD))
    base = (jnp.arange(DEPTH, dtype=jnp.int32) * BLOCK).astype(jnp.float32)[:, None] * frequency
    near = jnp.arange(BLOCK, dtype=jnp.int32).astype(jnp.float32)[:, None] * frequency
    return (
        jnp.stack([jnp.cos(base), jnp.sin(base)]),
        jnp.stack([jnp.cos(near), jnp.sin(near)]),
    )


def shards(ctx_size, tp_size, hidden, queries, key_weight, value_weight, parents, upstream):
    rows, width = hidden.shape
    depth_rows, key_width = key_weight.shape
    pair_width = 2 * key_width
    col_rows = depth_rows // ctx_size
    piece_rows = width // ctx_size
    chips = ctx_size // 2
    vmem = pl.BlockSpec(memory_space=pltpu.VMEM)
    anywhere = pl.BlockSpec(memory_space=pl.ANY)
    smem = pl.BlockSpec(memory_space=pltpu.SMEM)
    bf16, f32 = jnp.bfloat16, jnp.float32
    dma = pltpu.SemaphoreType.DMA
    base, near = rope_tables()
    split = (tp_size, ctx_size, piece_rows, key_width)

    out_types = (
        jax.ShapeDtypeStruct(queries.shape, bf16),
        jax.ShapeDtypeStruct(queries.shape, bf16),
        jax.ShapeDtypeStruct(hidden.shape, bf16),
        jax.ShapeDtypeStruct((col_rows, key_width), f32),
        jax.ShapeDtypeStruct((col_rows, key_width), f32),
    )
    return pl.pallas_call(
        partial(layer_kernel, ctx_size, tp_size),
        name="layer",
        out_shape=out_types,
        in_specs=[smem, vmem] + [anywhere] * 6 + [vmem] * 2,
        out_specs=(vmem,) * 5,
        scratch_shapes=[
            pltpu.VMEM((tp_size, 2, width // 2, rows), bf16),
            pltpu.VMEM((rows, pair_width), f32),
            pltpu.VMEM(key_weight.shape, bf16),
            pltpu.VMEM(key_weight.shape, bf16),
            pltpu.VMEM(queries.shape, bf16),
            pltpu.VMEM(queries.shape, bf16),
            pltpu.VMEM((ctx_size * rows // BLOCK, BLOCK, pair_width), bf16),
            pltpu.VMEM((ctx_size, col_rows, rows), bf16),
            pltpu.VMEM((rows, HD), f32),
            pltpu.VMEM((rows, HD), f32),
            pltpu.VMEM((ctx_size, tp_size - 1, 2, piece_rows, key_width), bf16),
            pltpu.VMEM((DEPTH // 2, 2 * BLOCK, width // key_width * BLOCK), f32),
            pltpu.VMEM((rows // BLOCK, DEPTH, BLOCK, pair_width), f32),
            pltpu.VMEM((chips, rows // BLOCK, BLOCK, pair_width), bf16),
            pltpu.VMEM((chips - 1, rows // BLOCK, BLOCK, pair_width), bf16),
            pltpu.VMEM((ctx_size, rows, pair_width), bf16),
            pltpu.VMEM((tp_size, rows, pair_width), bf16),
            dma((4,)),
            dma((2, 2, tp_size - 1)),
            dma((2, 2, tp_size - 1)),
            dma((ctx_size,)),
            dma((ctx_size,)),
            dma((tp_size, 2)),
            dma((tp_size, 2)),
        ]
        + [dma((chips,))] * 16
        + [dma((2, tp_size - 1))] * 2,
        compiler_params=pltpu.CompilerParams(
            collective_id=1, has_side_effects=True, vmem_limit_bytes=VMEM_LIMIT
        ),
    )(
        parents,
        hidden.T,
        key_weight,
        value_weight,
        key_weight.reshape(split),
        value_weight.reshape(split),
        queries,
        upstream,
        base,
        near,
    )


def solution(mesh):
    return jax.shard_map(
        partial(shards, mesh.shape["ctx"], mesh.shape["tp"]),
        mesh=mesh,
        in_specs=(
            P("ctx", "tp"),
            P("ctx", "tp"),
            P(None, "tp"),
            P(None, "tp"),
            P(),
            P("ctx", "tp"),
        ),
        out_specs=(P("ctx", "tp"),) * 5,
        check_vma=False,
    )
```

```python
from functools import partial
import math

import jax
import jax.numpy as jnp
from jax import lax
from jax.experimental import pallas as pl
from jax.experimental.pallas import tpu as pltpu
from jax.sharding import PartitionSpec as P

HD = 128
BLOCK = 128
DEPTH = 8
THETA = 1000000.0
NEGATIVE = -1e30
VMEM_LIMIT = 56 * 1024 * 1024
MESH = pl.DeviceIdType.MESH


def walk(parents_ref, block):
    chain = [block]
    for _ in range(DEPTH - 1):
        last = chain[-1]
        above = parents_ref[jnp.maximum(last, 0)]
        chain.append(jnp.where(last > 0, above, -1))
    depth = jnp.int32(0)
    for node in chain[1:]:
        depth = depth + jnp.where(node >= 0, 1, 0)
    path = []
    for level in range(DEPTH):
        found = jnp.int32(0)
        for hop in range(DEPTH):
            found = found + jnp.where(depth - hop == level, chain[hop], 0)
        path.append(found)
    return depth, path


def dot_f32(left, right, left_dim, right_dim):
    return lax.dot_general(
        left, right, (((left_dim,), (right_dim,)), ((), ())), preferred_element_type=jnp.float32
    )


def attend(parents_ref, kv_ref, q_ref, u_ref, att_ref, qg_ref, s_ref, grads_ref, release):
    rows, width = q_ref.shape
    blocks = rows // BLOCK
    pair_width = kv_ref.shape[2]
    key_width = pair_width // 2
    key_heads = key_width // HD
    groups = width // key_width
    lanes = groups * BLOCK
    step = 2 * BLOCK
    steps = DEPTH // 2
    scale = 1.0 / math.sqrt(HD)
    first = lax.axis_index("ctx") * blocks

    def one_block(b, carry):
        depth, path = walk(parents_ref, first + b)
        row0 = pl.multiple_of(b * BLOCK, BLOCK)
        here = pl.ds(row0, BLOCK)
        key_row = lax.broadcasted_iota(jnp.int32, (step, lanes), 0)
        query_row = lax.broadcasted_iota(jnp.int32, (step, lanes), 1) % BLOCK
        limit = depth * BLOCK + query_row - key_row
        for g in range(key_heads):
            def head_cols(h):
                return slice((g * groups + h) * HD, (g * groups + h + 1) * HD)

            key_cols = slice(g * HD, (g + 1) * HD)
            value_cols = slice(key_width + g * HD, key_width + (g + 1) * HD)
            q = jnp.concatenate([q_ref[here, head_cols(h)] for h in range(groups)], axis=0)
            u = jnp.concatenate([u_ref[here, head_cols(h)] for h in range(groups)], axis=0)
            u_t = u.astype(jnp.float32).T

            def pair(p, cols):
                return jnp.concatenate(
                    [
                        kv_ref[path[2 * p + i], :, cols] for i in range(2)
                    ],
                    axis=0,
                )

            top = jnp.full((1, lanes), NEGATIVE, jnp.float32)
            for p in range(steps):
                s = dot_f32(pair(p, key_cols), q, 1, 1) * scale
                s = jnp.where(limit >= p * step, s, NEGATIVE)
                s_ref[p] = s
                top = jnp.maximum(top, jnp.max(s, axis=0, keepdims=True))
            totals = jnp.zeros((1, lanes), jnp.float32)
            mixed = jnp.zeros((HD, lanes), jnp.float32)
            for p in range(steps):
                w = jnp.exp(s_ref[p] - top)
                s_ref[p] = w
                totals = totals + jnp.sum(w, axis=0, keepdims=True)
                mixed = mixed + dot_f32(pair(p, value_cols), w.astype(jnp.bfloat16), 0, 0)
            out_t = (mixed / totals).astype(jnp.bfloat16).astype(jnp.float32)
            out = out_t.T.astype(jnp.bfloat16)
            for h in range(groups):
                att_ref[here, head_cols(h)] = out[h * BLOCK : (h + 1) * BLOCK]
            deltas = jnp.sum(out_t * u_t, axis=0, keepdims=True)
            inverse = 1.0 / totals
            query_grad = jnp.zeros((HD, lanes), jnp.float32)
            for p in range(steps):
                prob = s_ref[p] * inverse
                value_part = dot_f32(prob.astype(jnp.bfloat16), u, 1, 0)
                prob_grad = dot_f32(pair(p, value_cols), u, 1, 1)
                ds = (prob * (prob_grad - deltas)).astype(jnp.bfloat16)
                key_part = dot_f32(ds, q, 1, 0) * scale
                query_grad = query_grad + dot_f32(pair(p, key_cols), ds, 0, 0)
                for i in range(2):
                    grads_ref[b, 2 * p + i, :, key_cols] = key_part[i * BLOCK : (i + 1) * BLOCK]
                    grads_ref[b, 2 * p + i, :, value_cols] = value_part[i * BLOCK : (i + 1) * BLOCK]
            qg = (query_grad * scale).T.astype(jnp.bfloat16)
            for h in range(groups):
                qg_ref[here, head_cols(h)] = qg[h * BLOCK : (h + 1) * BLOCK]
        return carry

    lax.fori_loop(0, blocks, one_block, 0)

    release()
    part_ref = kv_ref
    paths = [walk(parents_ref, first + b) for b in range(blocks)]
    block_total = part_ref.shape[0]

    def one_target(target, carry):
        total = jnp.zeros((BLOCK, pair_width), jnp.float32)
        for b in range(blocks):
            depth, path = paths[b]
            slot = jnp.int32(0)
            hits = jnp.int32(0)
            for level in range(DEPTH):
                hit = jnp.where((path[level] == target) & (depth >= level), 1, 0)
                slot = slot + hit * level
                hits = hits + hit
            total = total + grads_ref[b, slot] * hits.astype(jnp.float32)
        part_ref[target] = total.astype(part_ref.dtype)
        return carry

    lax.fori_loop(0, block_total, one_target, 0)


def remote(src, dst, send_sem, recv_sem, ctx, tp):
    return pltpu.make_async_remote_copy(
        src_ref=src,
        dst_ref=dst,
        send_sem=send_sem,
        recv_sem=recv_sem,
        device_id=(ctx, tp),
        device_id_type=MESH,
    )


def greet(devices, count):
    barrier = pltpu.get_barrier_semaphore()
    for ctx, tp, valid in devices:
        if valid is None:
            pl.semaphore_signal(barrier, inc=1, device_id=(ctx, tp), device_id_type=MESH)
        else:

            @pl.when(valid)
            def _():
                pl.semaphore_signal(barrier, inc=1, device_id=(ctx, tp), device_id_type=MESH)

    pl.semaphore_wait(barrier, count)


class PlaneGather:
    def __init__(self, buf, span, chips, relay, sems):
        me, tp = lax.axis_index("ctx"), lax.axis_index("tp")
        self.buf, self.span = buf, span
        self.chips, self.relay = chips, relay and chips == 4
        self.sems = sems
        self.me, self.tp = me, tp
        self.chip, self.core = me // 2, me % 2

    def slot(self, index):
        return self.buf.at[pl.ds(index * self.span, self.span)]

    def holder(self, offset):
        if self.relay:
            along_x = self.chip + (1 - 2 * (self.chip % 2) if offset % 2 else 0)
            return (along_x + (2 if offset >= 2 else 0)) % 4 * 2
        return (self.chip + self.chips - offset) % self.chips * 2

    def out_copy(self, offset):
        peer = (self.chip + offset) % self.chips * 2
        slot = self.slot(self.me)
        if self.relay:
            peer = self.holder(offset)
            if offset == 3:
                one, two = self.holder(1), self.holder(2)
                peer = two * (1 - self.core) + one * self.core
                slot = self.slot(one * (1 - self.core) + two * self.core + self.core)
        return remote(
            slot,
            slot,
            self.sems[0].at[offset],
            self.sems[1].at[offset],
            peer + self.core,
            self.tp,
        )

    def sib_copy(self, offset):
        slot = self.slot(self.holder(offset) + self.core)
        return remote(
            slot,
            slot,
            self.sems[2].at[offset],
            self.sems[3].at[offset],
            self.holder(0) + 1 - self.core,
            self.tp,
        )

    def start(self):
        for offset in range(1, 3 if self.relay else self.chips):
            self.out_copy(offset).start()
        self.sib_copy(0).start()

    def arrive(self, offset):
        self.out_copy(offset).wait_recv()
        if self.relay and offset < 3:

            @pl.when(self.core == offset - 1)
            def _():
                self.out_copy(3).start()

        self.sib_copy(offset).start()
        return self.holder(offset) + self.core

    def arrive_sibling(self, offset):
        self.sib_copy(offset).wait_recv()
        return self.holder(offset) + 1 - self.core

    def drain(self):
        for offset in range(self.chips):
            if offset:
                self.out_copy(offset).wait_send()
            self.sib_copy(offset).wait_send()


class Line:
    def __init__(self, slot_of, size, sems):
        self.ctx, self.tp = lax.axis_index("ctx"), lax.axis_index("tp")
        self.slot_of, self.size, self.sems = slot_of, size, sems

    def send(self, way, k):
        source = self.tp - k if way == 0 else self.tp + k
        valid = (
            (source >= 0) & (self.tp < self.size - 1)
            if way == 0
            else (source < self.size) & (self.tp > 0)
        )
        slot = self.slot_of(source)
        target = self.tp + 1 if way == 0 else self.tp - 1
        return valid, remote(
            slot, slot, self.sems[0].at[way, k], self.sems[1].at[way, k], self.ctx, target
        )

    def start(self, k):
        for way in range(2):
            valid, copy = self.send(way, k)

            @pl.when(valid)
            def _(copy=copy):
                copy.start()

    def arrive(self, k, then):
        for way in range(2):
            source = self.tp - 1 - k if way == 0 else self.tp + 1 + k
            valid = source >= 0 if way == 0 else source < self.size
            slot = self.slot_of(source)

            @pl.when(valid)
            def _(way=way, source=source, slot=slot):
                remote(
                    slot, slot, self.sems[0].at[way, k], self.sems[1].at[way, k], self.ctx, self.tp
                ).wait_recv()
                if k + 1 < self.size - 1:
                    on, copy = self.send(way, k + 1)

                    @pl.when(on)
                    def _():
                        copy.start()

                then(way, source)

    def drain(self):
        for k in range(self.size - 1):
            for way in range(2):
                valid, copy = self.send(way, k)

                @pl.when(valid)
                def _(copy=copy):
                    copy.wait_send()


def sum_grads(
    ctx_size,
    tp_size,
    part_ref,
    cos_ref,
    sin_ref,
    kw_ref,
    vw_ref,
    cols_ref,
    wall,
    weights,
    hg_ref,
    kwg_ref,
    vwg_ref,
    total,
    sib_buf,
    rs_buf,
    gbuf,
    zbuf,
    hg_acc,
    a_sems,
    b_sems,
    g_sems,
    z_sems,
    wait_columns,
    start_weights,
):
    me, tp = lax.axis_index("ctx"), lax.axis_index("tp")
    chips = ctx_size // 2
    chip, core = me // 2, me % 2
    rows, pair_width = total.shape
    blocks = sib_buf.shape[1]
    width = hg_ref.shape[1]
    strip = hg_acc.shape[2]
    key_width = pair_width // 2
    sibling = chip * 2 + 1 - core

    def sib_copy(offset):
        target = (chip + offset) % chips
        return remote(
            part_ref.at[pl.ds((target * 2 + 1 - core) * blocks, blocks)],
            sib_buf.at[offset],
            a_sems[0].at[offset],
            a_sems[1].at[offset],
            sibling,
            tp,
        )

    def chip_copy(offset):
        target = (chip + offset) % chips
        return remote(
            sib_buf.at[offset],
            rs_buf.at[offset - 1],
            b_sems[0].at[offset],
            b_sems[1].at[offset],
            target * 2 + core,
            tp,
        )

    order = list(range(1, chips)) + [0]
    for offset in order:
        sib_copy(offset).start()
    for offset in order:
        sib_copy(offset).wait_recv()
        own = part_ref[pl.ds(((chip + offset) % chips * 2 + core) * blocks, blocks)]
        both = own.astype(jnp.float32) + sib_buf[offset].astype(jnp.float32)
        if offset:
            sib_buf[offset] = both.astype(jnp.bfloat16)
            chip_copy(offset).start()
        else:
            total[...] = both.reshape(total.shape)
    for offset in range(1, chips):
        chip_copy(offset).wait_recv()
        total[...] += rs_buf[offset - 1].astype(jnp.float32).reshape(total.shape)
    cosine, sine = cos_ref[...], sin_ref[...]
    for g in range(key_width // HD):
        at = slice(g * HD, (g + 1) * HD)
        x = total[:, at]
        zbuf[tp, :, at] = (x * cosine - pltpu.roll(x, HD // 2, 1) * sine).astype(jnp.bfloat16)
    zbuf[tp, :, key_width:] = total[:, key_width:].astype(jnp.bfloat16)
    gbuf[me] = zbuf[tp]
    line = Line(lambda s: zbuf.at[s], tp_size, z_sems)
    line.start(0)
    grads = PlaneGather(gbuf, 1, chips, True, g_sems)
    grads.start()
    start_weights()

    def weight_grad(source, fresh=False):
        left = cols_ref[source]
        key_part = dot_f32(left, gbuf[source, :, :key_width], 1, 0)
        value_part = dot_f32(left, gbuf[source, :, key_width:], 1, 0)
        if fresh:
            kwg_ref[...] = key_part
            vwg_ref[...] = value_part
        else:
            kwg_ref[...] += key_part
            vwg_ref[...] += value_part

    def hidden_grad(source, key_rows, value_rows, fresh=False):
        for n in range(width // strip):
            at = slice(n * strip, (n + 1) * strip)
            part = dot_f32(zbuf[source, :, :key_width], key_rows[at], 1, 1) + dot_f32(
                zbuf[source, :, key_width:], value_rows[at], 1, 1
            )
            part = part.astype(jnp.bfloat16).astype(jnp.float32)
            hg_acc[n] = part if fresh else hg_acc[n] + part

    own = pl.ds(pl.multiple_of(tp * width, 128), width)
    for offset in range(1, ctx_size):
        wait_columns(offset)
    weight_grad(me, True)
    hidden_grad(tp, kw_ref[own, :], vw_ref[own, :], True)
    line.arrive(0, lambda way, source: None)
    for offset in range(1, chips):
        weight_grad(grads.arrive(offset))
        if offset < tp_size - 1:
            line.arrive(offset, lambda way, source: None)
        weights.arrive(offset)
    for k in range(chips, tp_size - 1):
        line.arrive(k, lambda way, source: None)
    for offset in range(chips):
        weight_grad(grads.arrive_sibling(offset))
    for offset in range(chips):
        weights.arrive_sibling(offset)

    def rows_of(j, matrix):
        pieces = [wall[c, j, matrix] for c in range(ctx_size)]
        if wall.shape[3] % 16:
            pieces = [piece.astype(jnp.float32) for piece in pieces]
        return jnp.concatenate(pieces, axis=0).astype(jnp.bfloat16)

    for j in range(tp_size - 1):
        source = (tp + 1 + j) % tp_size
        hidden_grad(source, rows_of(j, 0), rows_of(j, 1))
    for n in range(width // strip):
        hg_ref[:, n * strip : (n + 1) * strip] = hg_acc[n].astype(jnp.bfloat16)
    for offset in range(chips):
        sib_copy(offset).wait_send()
        if offset:
            chip_copy(offset).wait_send()
    grads.drain()
    weights.drain()
    line.drain()


def layer_kernel(
    ctx_size,
    tp_size,
    parents_ref,
    hid_ref,
    kw_hbm,
    vw_hbm,
    kw_any,
    vw_any,
    q_hbm,
    u_hbm,
    base_ref,
    near_ref,
    att_ref,
    qg_ref,
    hg_ref,
    kwg_ref,
    vwg_ref,
    feat,
    acc,
    kw_ref,
    vw_ref,
    q_ref,
    u_ref,
    kv_ref,
    cols_ref,
    cos_ref,
    sin_ref,
    wall,
    s_ref,
    slot_ref,
    sib_buf,
    rs_buf,
    gbuf,
    zbuf,
    load_sem,
    line_send,
    line_recv,
    col_send,
    col_recv,
    w_send,
    w_recv,
    kv_sems_0,
    kv_sems_1,
    kv_sems_2,
    kv_sems_3,
    wall_sems_0,
    wall_sems_1,
    wall_sems_2,
    wall_sems_3,
    a_sems_0,
    a_sems_1,
    b_sems_0,
    b_sems_1,
    g_sems_0,
    g_sems_1,
    g_sems_2,
    g_sems_3,
    z_send,
    z_recv,
):
    kv_sems = (kv_sems_0, kv_sems_1, kv_sems_2, kv_sems_3)
    wall_sems = (wall_sems_0, wall_sems_1, wall_sems_2, wall_sems_3)
    a_sems = (a_sems_0, a_sems_1)
    b_sems = (b_sems_0, b_sems_1)
    g_sems = (g_sems_0, g_sems_1, g_sems_2, g_sems_3)
    z_sems = (z_send, z_recv)
    me, tp = lax.axis_index("ctx"), lax.axis_index("tp")
    width, rows = hid_ref.shape
    loads = [
        pltpu.make_async_copy(source, held, load_sem.at[i])
        for i, (source, held) in enumerate(
            [(kw_hbm, kw_ref), (vw_hbm, vw_ref), (q_hbm, q_ref), (u_hbm, u_ref)]
        )
    ]
    for load in loads:
        load.start()
    half = width // 2
    key_width = kw_ref.shape[1]
    blocks = rows // BLOCK
    chips = ctx_size // 2
    col_rows = cols_ref.shape[1]
    per_half = half // col_rows
    greet(
        [((me + o) % ctx_size, tp, None) for o in range(1, ctx_size)]
        + [(me, (tp + o) % tp_size, None) for o in range(1, tp_size)],
        ctx_size + tp_size - 2,
    )
    for j in range(2):
        feat[tp, j] = hid_ref[j * half : (j + 1) * half, :]
    lines = [
        Line(lambda s, j=j: feat.at[s, j], tp_size, (line_send.at[j], line_recv.at[j]))
        for j in range(2)
    ]
    lines[0].start(0)

    def col_copy(source, j, i):
        dest = (source * 2 + j) * per_half + i
        offset = (dest + ctx_size - me) % ctx_size
        return dest, remote(
            feat.at[source, j, pl.ds(i * col_rows, col_rows), :],
            cols_ref.at[me],
            col_send.at[offset],
            col_recv.at[offset],
            dest,
            tp,
        )

    def share(source, j):
        for i in range(per_half):
            dest, copy = col_copy(source, j, i)

            @pl.when(dest != me)
            def _(copy=copy):
                copy.start()

            @pl.when(dest == me)
            def _(i=i):
                cols_ref[me] = feat[source, j, i * col_rows : (i + 1) * col_rows, :]

    def project(source, j):
        at = pl.ds(pl.multiple_of(source * width + j * half, 128), half)
        block = feat[source, j]
        acc[:, :key_width] += dot_f32(block, kw_ref[at, :], 0, 0)
        acc[:, key_width:] += dot_f32(block, vw_ref[at, :], 0, 0)

    def wait_columns(offset):
        source = (me + ctx_size - offset) % ctx_size
        slot = cols_ref.at[source]
        remote(slot, slot, col_send.at[offset], col_recv.at[offset], me, tp).wait()

    acc[...] = jnp.zeros_like(acc)
    lines[1].start(0)
    for j in range(2):
        share(tp, j)

    first = me * blocks
    lane = lax.broadcasted_iota(jnp.int32, (BLOCK, HD), 1)
    sign = jnp.where(lane < HD // 2, -1.0, 1.0)
    for b in range(blocks):
        depth, _ = walk(parents_ref, first + b)
        pick = lax.broadcasted_iota(jnp.int32, (DEPTH, HD), 0) == depth
        base_cos = jnp.sum(jnp.where(pick, base_ref[0], 0.0), axis=0, keepdims=True)
        base_sin = jnp.sum(jnp.where(pick, base_ref[1], 0.0), axis=0, keepdims=True)
        at = slice(b * BLOCK, (b + 1) * BLOCK)
        cos_ref[at, :] = base_cos * near_ref[0] - base_sin * near_ref[1]
        sin_ref[at, :] = (base_sin * near_ref[0] + base_cos * near_ref[1]) * sign

    for load in loads[:2]:
        load.wait()
    for j in range(2):
        project(tp, j)
    for j in range(2):
        for k in range(tp_size - 1):
            last = j == 1 and k == tp_size - 2

            def then(way, source, j=j, last=last):
                if not last:
                    share(source, j)
                project(source, j)

            lines[j].arrive(k, then)

    def piece_copy(offset, matrix):
        target = (tp + offset) % tp_size
        return remote(
            (kw_any, vw_any)[matrix].at[target, me],
            wall.at[me, tp_size - 1 - offset, matrix],
            w_send.at[offset, matrix],
            w_recv.at[offset, matrix],
            me,
            target,
        )

    for line in lines:
        line.drain()
    for offset in range(1, tp_size):
        for matrix in range(2):
            piece_copy(offset, matrix).start()

    cosine, sine = cos_ref[...], sin_ref[...]
    for g in range(key_width // HD):
        at = slice(g * HD, (g + 1) * HD)
        x = acc[:, at]
        keys = (x * cosine + pltpu.roll(x, HD // 2, 1) * sine).astype(jnp.bfloat16)
        for b in range(blocks):
            kv_ref[first + b, :, at] = keys[b * BLOCK : (b + 1) * BLOCK]
    for b in range(blocks):
        kv_ref[first + b, :, key_width:] = acc[
            b * BLOCK : (b + 1) * BLOCK, key_width:
        ].astype(jnp.bfloat16)
    gather = PlaneGather(kv_ref, blocks, chips, True, kv_sems)
    gather.start()
    for offset in range(1, chips):
        gather.arrive(offset)
    k = tp_size - 2
    for way in range(2):
        source = tp - 1 - k if way == 0 else tp + 1 + k
        valid = source >= 0 if way == 0 else source < tp_size

        @pl.when(valid)
        def _(source=source):
            share(source, 1)

    for offset in range(chips):
        gather.arrive_sibling(offset)
    weights = PlaneGather(wall, 1, chips, True, wall_sems)

    def start_weights():
        for offset in range(1, tp_size):
            for matrix in range(2):
                piece_copy(offset, matrix).wait()
        weights.start()

    for load in loads[2:]:
        load.wait()
    attend(parents_ref, kv_ref, q_ref, u_ref, att_ref, qg_ref, s_ref, slot_ref, gather.drain)
    sum_grads(
        ctx_size,
        tp_size,
        kv_ref,
        cos_ref,
        sin_ref,
        kw_ref,
        vw_ref,
        cols_ref,
        wall,
        weights,
        hg_ref,
        kwg_ref,
        vwg_ref,
        acc,
        sib_buf,
        rs_buf,
        gbuf,
        zbuf,
        s_ref,
        a_sems,
        b_sems,
        g_sems,
        z_sems,
        wait_columns,
        start_weights,
    )


def rope_tables():
    lane = jnp.arange(HD, dtype=jnp.int32) % (HD // 2)
    frequency = jnp.exp(lane.astype(jnp.float32) * (-2.0 * math.log(THETA) / HD))
    base = (jnp.arange(DEPTH, dtype=jnp.int32) * BLOCK).astype(jnp.float32)[:, None] * frequency
    near = jnp.arange(BLOCK, dtype=jnp.int32).astype(jnp.float32)[:, None] * frequency
    return (
        jnp.stack([jnp.cos(base), jnp.sin(base)]),
        jnp.stack([jnp.cos(near), jnp.sin(near)]),
    )


def shards(ctx_size, tp_size, hidden, queries, key_weight, value_weight, parents, upstream):
    rows, width = hidden.shape
    depth_rows, key_width = key_weight.shape
    pair_width = 2 * key_width
    col_rows = depth_rows // ctx_size
    piece_rows = width // ctx_size
    chips = ctx_size // 2
    vmem = pl.BlockSpec(memory_space=pltpu.VMEM)
    anywhere = pl.BlockSpec(memory_space=pl.ANY)
    smem = pl.BlockSpec(memory_space=pltpu.SMEM)
    bf16, f32 = jnp.bfloat16, jnp.float32
    dma = pltpu.SemaphoreType.DMA
    base, near = rope_tables()
    split = (tp_size, ctx_size, piece_rows, key_width)

    out_types = (
        jax.ShapeDtypeStruct(queries.shape, bf16),
        jax.ShapeDtypeStruct(queries.shape, bf16),
        jax.ShapeDtypeStruct(hidden.shape, bf16),
        jax.ShapeDtypeStruct((col_rows, key_width), f32),
        jax.ShapeDtypeStruct((col_rows, key_width), f32),
    )
    return pl.pallas_call(
        partial(layer_kernel, ctx_size, tp_size),
        name="layer",
        out_shape=out_types,
        in_specs=[smem, vmem] + [anywhere] * 6 + [vmem] * 2,
        out_specs=(vmem,) * 5,
        scratch_shapes=[
            pltpu.VMEM((tp_size, 2, width // 2, rows), bf16),
            pltpu.VMEM((rows, pair_width), f32),
            pltpu.VMEM(key_weight.shape, bf16),
            pltpu.VMEM(key_weight.shape, bf16),
            pltpu.VMEM(queries.shape, bf16),
            pltpu.VMEM(queries.shape, bf16),
            pltpu.VMEM((ctx_size * rows // BLOCK, BLOCK, pair_width), bf16),
            pltpu.VMEM((ctx_size, col_rows, rows), bf16),
            pltpu.VMEM((rows, HD), f32),
            pltpu.VMEM((rows, HD), f32),
            pltpu.VMEM((ctx_size, tp_size - 1, 2, piece_rows, key_width), bf16),
            pltpu.VMEM((DEPTH // 2, 2 * BLOCK, width // key_width * BLOCK), f32),
            pltpu.VMEM((rows // BLOCK, DEPTH, BLOCK, pair_width), f32),
            pltpu.VMEM((chips, rows // BLOCK, BLOCK, pair_width), bf16),
            pltpu.VMEM((chips - 1, rows // BLOCK, BLOCK, pair_width), bf16),
            pltpu.VMEM((ctx_size, rows, pair_width), bf16),
            pltpu.VMEM((tp_size, rows, pair_width), bf16),
            dma((4,)),
            dma((2, 2, tp_size - 1)),
            dma((2, 2, tp_size - 1)),
            dma((ctx_size,)),
            dma((ctx_size,)),
            dma((tp_size, 2)),
            dma((tp_size, 2)),
        ]
        + [dma((chips,))] * 16
        + [dma((2, tp_size - 1))] * 2,
        compiler_params=pltpu.CompilerParams(
            collective_id=1, has_side_effects=True, vmem_limit_bytes=VMEM_LIMIT
        ),
    )(
        parents,
        hidden.T,
        key_weight,
        value_weight,
        key_weight.reshape(split),
        value_weight.reshape(split),
        queries,
        upstream,
        base,
        near,
    )


def solution(mesh):
    return jax.shard_map(
        partial(shards, mesh.shape["ctx"], mesh.shape["tp"]),
        mesh=mesh,
        in_specs=(
            P("ctx", "tp"),
            P("ctx", "tp"),
            P(None, "tp"),
            P(None, "tp"),
            P(),
            P("ctx", "tp"),
        ),
        out_specs=(P("ctx", "tp"),) * 5,
        check_vma=False,
    )
```
